512 devices in a mesh: dp: 16 (over z_hi, x, core), seq: 32 (over z_lo, y).
Axes of the slice: x: 4, y: 8, z: 8 (z_hi: 2, z_lo: 4; z = z_hi * 4 + z_lo), core: 2. Of those that a mesh axis runs over, the one named last changes fastest.
Arguments:
- tokens: bfloat16 [16, 8192, 1536], P('dp', 'seq'), may hold values from -6 to 6
- cotangent: bfloat16 [16, 8192, 1536], P('dp', 'seq'), may hold values from -6 to 6
- conv_taps: bfloat16 [3, 1536], replicated, may hold values from -3 to 3
- block_mixes: bfloat16 [6, 256, 256], replicated, may hold values from -0.375 to 0.375
- gate_gain: float32 [1536], replicated, may hold values from 0.5 to 2
Outputs:
- input_grad: bfloat16 [16, 8192, 1536], P('dp', 'seq')
- mixes_grad: float32 [6, 256, 256], replicated
- taps_grad: float32 [3, 1536], replicated
- gain_grad: float32 [1536], replicated
The draws below stay inside these ranges and needn't reach their ends.
All inputs are finite; a program needn't handle non-finite values.
Results may differ from the reference program's by a relative error of at most 0.0076.
Values may be sent and summed in bfloat16 or wider, within the bound.
A program may use at most 64 MiB of HBM per device.

```python
import math
import jax
import jax.numpy as jnp
from jax import lax

D = 1536
TOK = 256
LENGTH = 8192
SLAB_COUNT = 16
N_SEQ = 32


def shard_levels(own_key, extent, pieces, least, high):
    gain, own = 1.0, jax.random.fold_in(own_key, 6)
    for position, blocks in pieces:
        heights = jnp.exp(jax.random.uniform(jax.random.fold_in(own, position), (blocks,), jnp.float32, least / len(pieces), high / len(pieces)))
        gain = gain * jnp.repeat(heights, extent[position] // blocks).reshape([-1 if axis == position else 1 for axis in range(len(extent))])
    return gain


def noise(stream_key, shape, scale, reach, cuts=(), kind=jnp.bfloat16):
    drawn = jax.random.normal(stream_key, shape, jnp.float32) * scale
    if len(cuts) > 0:
        drawn = shard_levels(stream_key, shape, cuts, -0.22, 0.18) * drawn
    return jnp.clip(drawn, min=-reach, max=reach).astype(kind)


def setup_inputs(seed: int = 0) -> dict:
    splits = jax.random.split(jax.random.key(seed), 6)
    tokens = noise(splits[0], (SLAB_COUNT, LENGTH, D), 1.0, 6.0, ((0, 16), (1, 32)))
    cotangent = noise(splits[1], (SLAB_COUNT, LENGTH, D), 1.0, 6.0, ((0, 16), (1, 32)))
    conv_taps = noise(splits[2], (3, D), 0.5, 3.0)
    block_mixes = noise(splits[3], (6, TOK, TOK), TOK ** -0.5, 0.375)
    gate_gain = jnp.clip(jnp.exp(jax.random.uniform(splits[4], (D,), jnp.float32, math.log(0.5), math.log(2.0))), 0.5, 2.0)
    return dict(tokens=tokens, cotangent=cotangent, conv_taps=conv_taps, block_mixes=block_mixes, gate_gain=gate_gain)


def block_mix(matrix, blocks):
    return jnp.einsum('ij,bjd->bid', matrix.astype(jnp.float32), blocks.astype(jnp.float32))

def mix_back(matrix, blocks):
    return jnp.einsum('ji,bjd->bid', matrix.astype(jnp.float32), blocks.astype(jnp.float32))

def outer_sum(left, right):
    return jnp.einsum('bid,bjd->ij', left.astype(jnp.float32), right.astype(jnp.float32))

def one_slab(tokens, cotangent, conv_taps, block_mixes, gate_gain):
    indices = jnp.arange(N_SEQ, dtype=jnp.int32)
    far_index = jnp.bitwise_xor(indices, jnp.int32(N_SEQ // 2))
    near_index = jnp.bitwise_xor(indices, jnp.int32(1))
    tap_weights = conv_taps.astype(jnp.float32)
    padded = jnp.pad(tokens, ((1, 1), (0, 0))).astype(jnp.float32)
    conv_out = (tap_weights[0] * padded[:-2] + tap_weights[1] * padded[1:-1] + tap_weights[2] * padded[2:]).astype(jnp.bfloat16)
    conv_blocks = conv_out.reshape(N_SEQ, TOK, D)
    first_mixed = block_mix(block_mixes[0], conv_blocks).astype(jnp.bfloat16)
    second_mixed = (block_mix(block_mixes[1], first_mixed) + block_mix(block_mixes[2], first_mixed[far_index])).astype(jnp.bfloat16)
    third_mixed = block_mix(block_mixes[3], second_mixed).astype(jnp.bfloat16)
    fourth_mixed = block_mix(block_mixes[4], third_mixed) + block_mix(block_mixes[5], third_mixed[near_index])
    token_blocks = tokens.reshape(N_SEQ, TOK, D).astype(jnp.float32)
    gate_in = gate_gain * token_blocks
    gate_sigmoid = jax.nn.sigmoid(gate_in)
    upstream = cotangent.reshape(N_SEQ, TOK, D).astype(jnp.float32)
    grad_fourth = (upstream * gate_in * gate_sigmoid).astype(jnp.bfloat16)
    grad_gate = upstream * fourth_mixed * gate_sigmoid * (1.0 + gate_in * (1.0 - gate_sigmoid))
    gain_term = lax.optimization_barrier(jnp.sum(grad_gate * token_blocks, axis=(0, 1)))
    grad_third = (mix_back(block_mixes[4], grad_fourth) + mix_back(block_mixes[5], grad_fourth[near_index])).astype(jnp.bfloat16)
    grad_second = mix_back(block_mixes[3], grad_third).astype(jnp.bfloat16)
    grad_first = (mix_back(block_mixes[1], grad_second) + mix_back(block_mixes[2], grad_second[far_index])).astype(jnp.bfloat16)
    grad_conv = mix_back(block_mixes[0], grad_first).astype(jnp.bfloat16)
    mix_terms = jnp.stack([outer_sum(grad_first, conv_blocks), outer_sum(grad_second, first_mixed), outer_sum(grad_second, first_mixed[far_index]), outer_sum(grad_third, second_mixed), outer_sum(grad_fourth, third_mixed), outer_sum(grad_fourth, third_mixed[near_index])])
    grad_flat = grad_conv.reshape(LENGTH, D).astype(jnp.float32)
    taps_term = jnp.stack([lax.optimization_barrier(jnp.sum(grad_flat * padded[:-2], axis=0)), lax.optimization_barrier(jnp.sum(grad_flat * padded[1:-1], axis=0)), lax.optimization_barrier(jnp.sum(grad_flat * padded[2:], axis=0))])
    grad_padded = jnp.pad(grad_flat, ((1, 1), (0, 0)))
    input_grad = (tap_weights[0] * grad_padded[2:] + tap_weights[1] * grad_padded[1:-1] + tap_weights[2] * grad_padded[:-2] + grad_gate.reshape(LENGTH, D) * gate_gain).astype(jnp.bfloat16)
    return (input_grad, mix_terms, taps_term, gain_term)

def reference(tokens, cotangent, conv_taps, block_mixes, gate_gain):

    def per_slab(slab_pair):
        return one_slab(slab_pair[0], slab_pair[1], conv_taps, block_mixes, gate_gain)
    input_grad, mix_terms, taps_terms, gain_terms = lax.map(per_slab, (tokens, cotangent))
    mix_scale = 1.0 / math.sqrt(SLAB_COUNT * N_SEQ * D)
    tok_scale = 1.0 / math.sqrt(SLAB_COUNT * LENGTH)
    mixes_grad = lax.optimization_barrier(jnp.sum(mix_terms, axis=0)) * mix_scale
    taps_grad = lax.optimization_barrier(jnp.sum(taps_terms, axis=0)) * tok_scale
    gain_grad = lax.optimization_barrier(jnp.sum(gain_terms, axis=0)) * tok_scale
    return (input_grad, mixes_grad, taps_grad, gain_grad)
```

```python
import functools
import math

import jax
import jax.numpy as jnp
from jax import lax
from jax.experimental import pallas as pl
from jax.experimental.pallas import tpu as pltpu
from jax.sharding import PartitionSpec as P

F32, BF16 = jnp.float32, jnp.bfloat16
MESH = pl.DeviceIdType.MESH

CORES, XS, YS, ZLO, ZHI = 2, 4, 8, 4, 2
ZS = ZLO * ZHI
T, D = 256, 1536
QUARTER = D // 4
LANES = 128
CHUNKS = QUARTER // LANES
WIDE = 4 * LANES
EDGE = 16
TILE = 16
ROWS = 6 * T * T // LANES
HALF, PX, PY = ROWS // CORES, ROWS // (CORES * XS), ROWS // (CORES * XS * YS)


def far(v):
    return jnp.concatenate([v[:, 2 * LANES :], v[:, : 2 * LANES]], axis=1)


def near(v):
    a, b, c, d = (v[:, i * LANES : (i + 1) * LANES] for i in range(4))
    return jnp.concatenate([b, a, d, c], axis=1)


def mm(a, b):
    return jnp.dot(a, b, preferred_element_type=F32)


def mm_nt(a, b):
    return lax.dot_general(a, b, (((1,), (1,)), ((), ())), preferred_element_type=F32)


def kernel(
    tok_hbm, cot_hbm, taps_ref, mixes_ref, gain_ref,
    out_hbm, ag, e_out,
    tok, cot, halo, pad, conv, gf2, h, f2, t2, s2, gt, gs2, g1, fourth,
    gcpad, ggg, outb, edge_out, edges, wts,
    m0, m12, m3, m45, m0t, m12t, m3t, m45t,
    grads, own_x, own_y, core_out, core_in, x_out, x_in, y_out, y_in, z_in,
    e_own, e_core, e_x, e_y, e_z,
    in_send, in_recv, in_local, halo_send, halo_recv, edge_send, edge_recv,
    out_send, out_recv, out_local, core_sem, x_send, x_recv, y_send, y_recv,
    z_send, z_recv, gy_send, gy_recv, gx_send, gx_recv, gc_send, gc_recv,
    ec_sem, ex_send, ex_recv, ey_send, ey_recv, ez_send, ez_recv, eq_send, eq_recv,
):
    dp, k = lax.axis_index("dp"), lax.axis_index("seq")
    core, x, z_hi = lax.rem(dp, CORES), lax.rem(lax.div(dp, CORES), XS), lax.div(dp, CORES * XS)
    y, z_lo = lax.rem(k, YS), lax.div(k, YS)
    z = z_hi * ZLO + z_lo
    yb, yp = lax.rem(y, 2), lax.div(y, 2)
    zb, zp = lax.div(z_lo, 2), lax.rem(z_lo, 2)
    q = yb + 2 * zb

    def at(core_=core, x_=x, y_=y, z_=z):
        return (lax.div(z_, ZLO) * (XS * CORES) + x_ * CORES + core_, lax.rem(z_, ZLO) * YS + y_)

    def in_group(yp_, zp_, quarter):
        return (dp, (zp_ + 2 * lax.div(quarter, 2)) * YS + 2 * yp_ + lax.rem(quarter, 2))

    last_y, first_y = yp == YS // 2 - 1, yp == 0
    next_yp, next_zp = lax.rem(yp + 1, YS // 2), jnp.where(last_y, 1 - zp, zp)
    prev_yp, prev_zp = lax.rem(yp + YS // 2 - 1, YS // 2), jnp.where(first_y, 1 - zp, zp)
    next_flip = jnp.where(last_y, zp, 0)
    prev_flip = jnp.where(first_y, 1 - zp, 0)
    has_prev = 1.0 - prev_flip.astype(F32)
    has_next = 1.0 - next_flip.astype(F32)

    mates = [lax.rem(q + m, 4) for m in range(1, 4)]

    def rcopy(src, dst, send, recv, device):
        return pltpu.make_async_remote_copy(
            src_ref=src, dst_ref=dst, send_sem=send, recv_sem=recv, device_id=device, device_id_type=MESH
        )

    def lanes(quarter, c):
        return pl.ds(pl.multiple_of(quarter * QUARTER + c * LANES, LANES), LANES)

    barrier = pltpu.get_barrier_semaphore()
    others = [in_group(yp, zp, m) for m in mates]
    others += [in_group(next_yp, next_zp, m) for m in range(4)]
    others += [in_group(prev_yp, prev_zp, m) for m in range(4)]
    others += [at(core_=1 - core)]
    others += [at(x_=lax.rem(x + i, XS)) for i in range(1, XS)]
    others += [at(y_=lax.rem(y + i, YS)) for i in range(1, YS)]
    others += [at(z_=lax.rem(z + i, ZS)) for i in range(1, ZS)]
    for device in others:
        pl.semaphore_signal(barrier, inc=1, device_id=device, device_id_type=MESH)
    pl.semaphore_wait(barrier, len(others))

    halo_yp, halo_zp = jnp.where(yb == 1, next_yp, prev_yp), jnp.where(yb == 1, next_zp, prev_zp)
    halo_flip = jnp.where(yb == 1, next_flip, prev_flip)
    halo_half = lax.rem(zb + halo_flip, 2)
    halo_slot = (1 - yb) * 2 + halo_half
    halo_row = pl.multiple_of(yb * (T - EDGE), EDGE)
    halo_copies = [
        rcopy(
            tok_hbm.at[pl.ds(halo_row, EDGE), pl.ds(m * QUARTER, QUARTER)],
            halo.at[halo_slot],
            halo_send.at[m],
            halo_recv.at[halo_slot],
            in_group(halo_yp, halo_zp, m),
        )
        for m in range(4)
    ]
    for copy in halo_copies:
        copy.start()

    def inbound(c, arrays=(0, 1)):
        copies = []
        for m in (1, 2, 0):
            for a in arrays:
                src, dst = ((tok_hbm, tok), (cot_hbm, cot))[a]
                copies.append(
                    rcopy(
                        src.at[:, lanes(mates[m], c)],
                        dst.at[c, q],
                        in_send.at[a, c, m],
                        in_recv.at[a, c, 2 - m],
                        in_group(yp, zp, mates[m]),
                    )
                )
        return copies

    def local(c):
        return [
            pltpu.make_async_copy(src.at[:, lanes(q, c)], dst.at[c, q], in_local.at[a, c])
            for a, (src, dst) in enumerate(((tok_hbm, tok), (cot_hbm, cot)))
        ]

    for c in range(CHUNKS):
        for copy in inbound(c) + local(c):
            copy.start()

    def transposed(v):
        return v.astype(F32).T.astype(BF16)

    m0[...] = mixes_ref[0]
    m12[:, :T], m12[:, T:] = mixes_ref[1], mixes_ref[2]
    m3[...] = mixes_ref[3]
    m45[:, :T], m45[:, T:] = mixes_ref[4], mixes_ref[5]
    m0t[...] = transposed(mixes_ref[0])
    m12t[:, :T], m12t[:, T:] = transposed(mixes_ref[1]), transposed(mixes_ref[2])
    m3t[...] = transposed(mixes_ref[3])
    m45t[:, :T], m45t[:, T:] = transposed(mixes_ref[4]), transposed(mixes_ref[5])
    wts[0:3, :] = taps_ref[...].astype(F32)
    wts[3:4, :] = gain_ref[...]
    grads[...] = jnp.zeros_like(grads)
    e_own[...] = jnp.zeros_like(e_own)

    def weights(c):
        w = wts[:, lanes(q, c)]
        w = jnp.concatenate([w] * 4, axis=1)
        return [w[i : i + 1] for i in range(4)]

    def fill_edges(ref, prev, nxt):
        body = ref[8 : 16, :], ref[T : T + 8, :]
        first, last = body[0][0:1], body[1][7:8]
        ref[7:8, :] = jnp.concatenate([prev[0], last[:, :LANES], prev[1], last[:, 2 * LANES : 3 * LANES]], axis=1)
        ref[T + 8 : T + 9, :] = jnp.concatenate(
            [first[:, LANES : 2 * LANES], nxt[0], first[:, 3 * LANES :], nxt[1]], axis=1
        )

    def mask_edges(prev, nxt):
        return [prev[0] * has_prev, prev[1]], [nxt[0], nxt[1] * has_next]

    def tile_rows(i):
        return pl.ds(pl.multiple_of(i * TILE, TILE), TILE)

    def window(ref, i):
        w = ref[pl.ds(pl.multiple_of(i * TILE, TILE), TILE + 16), :]
        return w[7 : 7 + TILE], w[8 : 8 + TILE], w[9 : 9 + TILE]

    def edge_copies(c):
        copies = []
        for half in range(2):
            for side, (yp_, zp_, flip) in enumerate(((next_yp, next_zp, next_flip), (prev_yp, prev_zp, prev_flip))):
                slot = side * 2 + lax.rem(half + flip, 2)
                copies.append(
                    rcopy(
                        edge_out.at[c, side * 2 + half],
                        edges.at[c, slot],
                        edge_send.at[c, side * 2 + half],
                        edge_recv.at[c, slot],
                        in_group(yp_, zp_, q),
                    )
                )
        return copies

    def edge_wait(c):
        for slot in range(4):
            rcopy(
                edge_out.at[c, slot], edges.at[c, slot], edge_send.at[c, slot], edge_recv.at[c, slot],
                in_group(next_yp, next_zp, q),
            ).wait_recv()

    def wait_inbound(c):
        for a in range(2):
            dst = (tok, cot)[a]
            for m in range(3):
                rcopy(
                    dst.at[c, q], dst.at[c, mates[m]], in_send.at[a, c, m], in_recv.at[a, c, m],
                    in_group(yp, zp, mates[m]),
                ).wait_recv()
        for copy in local(c):
            copy.wait()

    def chain(c):
        for b in range(4):
            pad[8 : 8 + T, b * LANES : (b + 1) * LANES] = tok[c, b].astype(F32)
        chunk = pl.ds(pl.multiple_of(c * LANES, LANES), LANES)
        ends = [halo[s, :, chunk].astype(F32) for s in range(4)]
        fill_edges(
            pad, *mask_edges([ends[0][EDGE - 1 :], ends[1][EDGE - 1 :]], [ends[2][:1], ends[3][:1]])
        )
        w = weights(c)

        def before(i, carry):
            prev, cur, nxt = window(pad, i)
            rows = tile_rows(i)
            conv[rows, :] = (w[0] * prev + w[1] * cur + w[2] * nxt).astype(BF16)
            up = jnp.concatenate([cot[c, b, rows, :] for b in range(4)], axis=1).astype(F32)
            gate = w[3] * cur
            sig = 1.0 / (1.0 + jnp.exp(-gate))
            gf = (up * gate * sig).astype(BF16)
            gf2[rows, :] = gf
            gf2[pl.ds(pl.multiple_of(T + i * TILE, TILE), TILE), :] = near(gf)
            h[rows, :] = up * sig * (1.0 + gate * (1.0 - sig))
            return carry

        lax.fori_loop(0, T // TILE, before, 0)

        first = mm(m0[...], conv[...]).astype(BF16)
        f2[:T, :], f2[T:, :] = first, far(first)
        third_grad = mm(m45t[...], gf2[...]).astype(BF16)
        gt[...] = third_grad
        s2[...] = mm(m12[...], f2[...]).astype(BF16)
        second_grad = mm(m3t[...], gt[...]).astype(BF16)
        gs2[:T, :], gs2[T:, :] = second_grad, far(second_grad)
        third = mm(m3[...], s2[...]).astype(BF16)
        t2[:T, :], t2[T:, :] = third, near(third)
        g1[...] = mm(m12t[...], gs2[...]).astype(BF16)
        fourth[...] = mm(m45[...], t2[...])
        gc = mm(m0t[...], g1[...]).astype(BF16)
        gcpad[c, 8 : 8 + T, :] = gc.astype(F32)
        for half in range(2):
            odd = slice((2 * half + 1) * LANES, (2 * half + 2) * LANES)
            even = slice(2 * half * LANES, (2 * half + 1) * LANES)
            edge_out[c, half] = gc[T - EDGE :, odd]
            edge_out[c, 2 + half] = gc[:EDGE, even]
        for copy in edge_copies(c):
            copy.start()

        def add_grad(i, value):
            grads[2 * i * T : (2 * i + 1) * T, :] += value[:, :LANES]
            grads[(2 * i + 1) * T : (2 * i + 2) * T, :] += value[:, LANES:]

        add_grad(0, mm_nt(g1[...], conv[...]))
        add_grad(3, mm_nt(gt[...], s2[...]))
        both = mm_nt(gs2[:T, :], f2[...])
        add_grad(1, both[:, :T])
        add_grad(2, both[:, T:])
        both = mm_nt(gf2[:T, :], t2[...])
        add_grad(4, both[:, :T])
        add_grad(5, both[:, T:])

    def sums(c):
        w = weights(c)

        def after(i, carry):
            prev, cur, nxt = window(pad, i)
            rows = tile_rows(i)
            gg = h[rows, :] * fourth[rows, :]
            gc = gcpad[c, pl.ds(pl.multiple_of(8 + i * TILE, 8), TILE), :]
            ggg[c, rows, :] = gg * w[3]

            def fold(v):
                return v[:8] + v[8:]

            return tuple(
                have + fold(v) for have, v in zip(carry, (gc * prev, gc * cur, gc * nxt, gg * cur))
            )

        zero = jnp.zeros((8, WIDE), F32)
        totals = lax.fori_loop(0, T // TILE, after, (zero,) * 4)
        for j, total in enumerate(totals):
            row = jnp.sum(total, axis=0, keepdims=True)
            e_own[c, j : j + 1, :] = sum(row[:, b * LANES : (b + 1) * LANES] for b in range(4))

    def finish(c):
        edge_wait(c)
        ends = [edges[c, s].astype(F32) for s in range(4)]
        fill_edges(
            gcpad.at[c], *mask_edges([ends[0][EDGE - 1 :], ends[1][EDGE - 1 :]], [ends[2][:1], ends[3][:1]])
        )
        w = weights(c)

        def close(i, carry):
            prev, cur, nxt = window(gcpad.at[c], i)
            rows = tile_rows(i)
            out = (w[0] * nxt + w[1] * cur + w[2] * prev + ggg[c, rows, :]).astype(BF16)
            for b in range(4):
                outb[c, b, rows, :] = out[:, b * LANES : (b + 1) * LANES]
            return carry

        lax.fori_loop(0, T // TILE, close, 0)

    def outbound(c):
        return [
            rcopy(
                outb.at[c, mates[m]],
                out_hbm.at[:, lanes(q, c)],
                out_send.at[c, m],
                out_recv.at[c, 2 - m],
                in_group(yp, zp, mates[m]),
            )
            for m in (1, 2, 0)
        ]

    def out_own(c):
        return pltpu.make_async_copy(outb.at[c, q], out_hbm.at[:, lanes(q, c)], out_local.at[c])

    def send_out(c):
        for copy in outbound(c):
            copy.start()
        out_own(c).start()

    for slot in range(4):
        rcopy(
            tok_hbm.at[pl.ds(0, EDGE), pl.ds(0, QUARTER)], halo.at[slot], halo_send.at[slot], halo_recv.at[slot],
            in_group(next_yp, next_zp, q),
        ).wait_recv()

    def step(c, carry):
        @pl.when(c > 0)
        def _():
            sums(c - 1)
            finish(c - 1)

        wait_inbound(c)

        @pl.when(c == CHUNKS - 1)
        def _():
            for past in range(CHUNKS - 1):
                send_out(past)

        chain(c)
        return carry

    lax.fori_loop(0, CHUNKS, step, 0)

    sibling = at(core_=1 - core)
    x_mates = [lax.rem(x + i, XS) for i in range(1, XS)]
    y_mates = [lax.rem(y + i, YS) for i in range(1, YS)]
    z_mates = [lax.rem(z + i, ZS) for i in range(1, ZS)]

    def rows_of(start, size):
        return pl.ds(pl.multiple_of(start, EDGE), size)

    core_out[...] = grads[rows_of((1 - core) * HALF, HALF), :].astype(BF16)
    core_copy = rcopy(core_out, core_in, core_sem.at[0], core_sem.at[1], sibling)
    core_copy.start()
    sums(CHUNKS - 1)
    e_core_copy = rcopy(e_own, e_core, ec_sem.at[0], ec_sem.at[1], sibling)
    e_core_copy.start()
    core_copy.wait_recv()
    x_copies = []
    for i, other in enumerate(x_mates):
        part = grads[rows_of(core * HALF + other * PX, PX), :] + core_in[rows_of(other * PX, PX), :].astype(F32)
        x_out[i] = part.astype(BF16)
        x_copies.append(rcopy(x_out.at[i], x_in.at[i], x_send.at[i], x_recv.at[i], at(x_=other)))
        x_copies[-1].start()
    own_x[...] = grads[rows_of(core * HALF + x * PX, PX), :] + core_in[rows_of(x * PX, PX), :].astype(F32)

    e_core_copy.wait_recv()
    e_x[x] = e_own[...] + e_core[...]
    ex_copies = [
        rcopy(e_x.at[x], e_x.at[x], ex_send.at[i], ex_recv.at[i], at(x_=other)) for i, other in enumerate(x_mates)
    ]
    for copy in ex_copies:
        copy.start()

    finish(CHUNKS - 1)
    send_out(CHUNKS - 1)

    for copy in x_copies:
        copy.wait_recv()
    own_x[...] += x_in[0].astype(F32) + x_in[1].astype(F32) + x_in[2].astype(F32)
    y_out[...] = own_x[...].astype(BF16)
    y_copies = [
        rcopy(y_out.at[rows_of(other * PY, PY)], y_in.at[i], y_send.at[i], y_recv.at[i], at(y_=other))
        for i, other in enumerate(y_mates)
    ]
    for copy in y_copies:
        copy.start()

    def slot_wait(ref, slot, send, recv, device):
        rcopy(ref.at[slot], ref.at[slot], send, recv, device).wait_recv()

    for i in range(XS - 1):
        slot_wait(e_x, lax.rem(x + XS - 1 - i, XS), ex_send.at[i], ex_recv.at[i], sibling)
    e_y[yp] = e_x[0] + e_x[1] + e_x[2] + e_x[3]
    ey_copies = [
        rcopy(e_y.at[yp], e_y.at[yp], ey_send.at[i], ey_recv.at[i], at(y_=lax.rem(y + 2 * (i + 1), YS)))
        for i in range(3)
    ]
    for copy in ey_copies:
        copy.start()

    for copy in y_copies:
        copy.wait_recv()
    total = own_x[rows_of(y * PY, PY), :]
    for i in range(YS - 1):
        total = total + y_in[i].astype(F32)
    z_in[z] = total.astype(BF16)
    z_copies = [
        rcopy(z_in.at[z], z_in.at[z], z_send.at[i], z_recv.at[i], at(z_=other)) for i, other in enumerate(z_mates)
    ]
    for copy in z_copies:
        copy.start()

    for i in range(3):
        slot_wait(e_y, lax.rem(yp + 3 - i, 4), ey_send.at[i], ey_recv.at[i], sibling)
    ez_me = z_hi * 2 + zp
    e_z[ez_me] = e_y[0] + e_y[1] + e_y[2] + e_y[3]

    def ez_device(slot):
        return at(z_=lax.div(slot, 2) * ZLO + 2 * zb + lax.rem(slot, 2))

    ez_copies = [
        rcopy(e_z.at[ez_me], e_z.at[ez_me], ez_send.at[i], ez_recv.at[i], ez_device(lax.rem(ez_me + i + 1, 4)))
        for i in range(3)
    ]
    for copy in ez_copies:
        copy.start()

    for i in range(ZS - 1):
        slot_wait(z_in, lax.rem(z + ZS - 1 - i, ZS), z_send.at[i], z_recv.at[i], sibling)
    total = z_in[0].astype(F32)
    for i in range(1, ZS):
        total = total + z_in[i].astype(F32)
    own = rows_of(core * HALF + x * PX + y * PY, PY)
    ag[own, :] = total.astype(BF16)
    gy_copies = [
        rcopy(ag.at[own], ag.at[own], gy_send.at[i], gy_recv.at[i], at(y_=other)) for i, other in enumerate(y_mates)
    ]
    for copy in gy_copies:
        copy.start()

    for i in range(3):
        slot_wait(e_z, lax.rem(ez_me + 3 - i, 4), ez_send.at[i], ez_recv.at[i], sibling)
    e_out[q] = e_z[0] + e_z[1] + e_z[2] + e_z[3]
    eq_copies = [
        rcopy(e_out.at[q], e_out.at[q], eq_send.at[i], eq_recv.at[i], in_group(yp, zp, mates[i])) for i in range(3)
    ]
    for copy in eq_copies:
        copy.start()

    for i in range(YS - 1):
        there = rows_of(core * HALF + x * PX + lax.rem(y + YS - 1 - i, YS) * PY, PY)
        rcopy(ag.at[there], ag.at[there], gy_send.at[i], gy_recv.at[i], sibling).wait_recv()
    mine = rows_of(core * HALF + x * PX, PX)
    gx_copies = [
        rcopy(ag.at[mine], ag.at[mine], gx_send.at[i], gx_recv.at[i], at(x_=other)) for i, other in enumerate(x_mates)
    ]
    for copy in gx_copies:
        copy.start()
    gc_copies = [rcopy(ag.at[mine], ag.at[mine], gc_send.at[0], gc_recv.at[0], sibling)]
    gc_copies[0].start()
    for i in range(XS - 1):
        there = rows_of(core * HALF + lax.rem(x + XS - 1 - i, XS) * PX, PX)
        rcopy(ag.at[there], ag.at[there], gx_send.at[i], gx_recv.at[i], sibling).wait_recv()
        gc_copies.append(rcopy(ag.at[there], ag.at[there], gc_send.at[i + 1], gc_recv.at[i + 1], sibling))
        gc_copies[-1].start()

    for i in range(3):
        slot_wait(e_out, mates[2 - i], eq_send.at[i], eq_recv.at[i], sibling)
    for c in range(CHUNKS):
        for m in range(3):
            rcopy(
                outb.at[c, mates[m]], out_hbm.at[:, lanes(mates[m], c)], out_send.at[c, m], out_recv.at[c, m], sibling
            ).wait_recv()
        out_own(c).wait()
    for i in range(XS):
        there = rows_of((1 - core) * HALF + lax.rem(x + XS - i, XS) * PX, PX)
        rcopy(ag.at[there], ag.at[there], gc_send.at[i], gc_recv.at[i], sibling).wait_recv()
    sent = halo_copies + [core_copy, e_core_copy] + x_copies + ex_copies + y_copies + ey_copies
    sent += z_copies + ez_copies + gy_copies + eq_copies + gx_copies + gc_copies
    for c in range(CHUNKS):
        sent += inbound(c) + edge_copies(c) + outbound(c)
    for copy in sent:
        copy.wait_send()


def local(tokens, cotangent, conv_taps, block_mixes, gate_gain):
    slabs = lax.axis_size("dp")
    tok_scale = 1.0 / math.sqrt(slabs * lax.axis_size("seq") * T)
    mix_scale = 1.0 / math.sqrt(slabs * lax.axis_size("seq") * D)
    small = (CHUNKS, 8, LANES)
    dma = pltpu.SemaphoreType.DMA
    wide = (T, WIDE)
    scratch = [
        *[pltpu.VMEM((CHUNKS, 4, T, LANES), BF16)] * 2,
        pltpu.VMEM((4, EDGE, QUARTER), BF16),
        pltpu.VMEM((T + 16, WIDE), F32),
        pltpu.VMEM(wide, BF16),
        pltpu.VMEM((2 * T, WIDE), BF16),
        pltpu.VMEM(wide, F32),
        pltpu.VMEM((2 * T, WIDE), BF16),
        pltpu.VMEM((2 * T, WIDE), BF16),
        pltpu.VMEM(wide, BF16),
        pltpu.VMEM(wide, BF16),
        pltpu.VMEM((2 * T, WIDE), BF16),
        pltpu.VMEM(wide, BF16),
        pltpu.VMEM(wide, F32),
        pltpu.VMEM((CHUNKS, T + 16, WIDE), F32),
        pltpu.VMEM((CHUNKS, T, WIDE), F32),
        pltpu.VMEM((CHUNKS, 4, T, LANES), BF16),
        *[pltpu.VMEM((CHUNKS, 4, EDGE, LANES), BF16)] * 2,
        pltpu.VMEM((8, D), F32),
        *[pltpu.VMEM((T, n * T), BF16) for n in (1, 2, 1, 2, 1, 2, 1, 2)],
        pltpu.VMEM((ROWS, LANES), F32),
        pltpu.VMEM((PX, LANES), F32),
        pltpu.VMEM((PY, LANES), F32),
        *[pltpu.VMEM((HALF, LANES), BF16)] * 2,
        *[pltpu.VMEM((XS - 1, PX, LANES), BF16)] * 2,
        pltpu.VMEM((PX, LANES), BF16),
        pltpu.VMEM((YS - 1, PY, LANES), BF16),
        pltpu.VMEM((ZS, PY, LANES), BF16),
        *[pltpu.VMEM(small, F32)] * 2,
        *[pltpu.VMEM((4, *small), F32)] * 3,
        *[dma((2, CHUNKS, 3))] * 2, dma((2, CHUNKS)),
        *[dma((4,))] * 2,
        *[dma((CHUNKS, 4))] * 2,
        *[dma((CHUNKS, 3))] * 2, dma((CHUNKS,)),
        dma((2,)),
        *[dma((XS - 1,))] * 2,
        *[dma((YS - 1,))] * 2,
        *[dma((ZS - 1,))] * 2,
        *[dma((YS - 1,))] * 2,
        *[dma((XS - 1,))] * 2,
        *[dma((XS,))] * 2,
        dma((2,)),
        *[dma((3,))] * 8,
    ]
    vmem, hbm = pl.BlockSpec(memory_space=pltpu.VMEM), pl.BlockSpec(memory_space=pl.ANY)
    flops = 18 * 2 * T * T * D
    input_grad, mixes, small_sums = pl.pallas_call(
        kernel,
        out_shape=(
            jax.ShapeDtypeStruct((T, D), BF16),
            jax.ShapeDtypeStruct((ROWS, LANES), BF16),
            jax.ShapeDtypeStruct((4, *small), F32),
        ),
        in_specs=[hbm, hbm, vmem, vmem, vmem],
        out_specs=(hbm, vmem, vmem),
        scratch_shapes=scratch,
        compiler_params=pltpu.CompilerParams(
            collective_id=0, has_side_effects=True, vmem_limit_bytes=44 * 1024 * 1024
        ),
        cost_estimate=pl.CostEstimate(flops=flops, bytes_accessed=6 * T * D, transcendentals=T * D),
    )(tokens[0], cotangent[0], conv_taps, block_mixes, gate_gain[None])
    mixes_grad = mixes.reshape(6, 2, T, LANES).transpose(0, 2, 1, 3).reshape(6, T, T).astype(F32) * mix_scale
    rows = small_sums[:, :, :4].transpose(2, 0, 1, 3).reshape(4, D) * tok_scale
    return input_grad[None], mixes_grad, rows[:3], rows[3]


def solution(mesh):
    placed = (P("dp", "seq", None), P("dp", "seq", None), P(), P(), P())
    return jax.shard_map(
        local,
        mesh=mesh,
        in_specs=placed,
        out_specs=(P("dp", "seq", None), P(), P(), P()),
        check_vma=False,
    )
```

```python
import functools
import math

import jax
import jax.numpy as jnp
from jax import lax
from jax.experimental import pallas as pl
from jax.experimental.pallas import tpu as pltpu
from jax.sharding import PartitionSpec as P

F32, BF16 = jnp.float32, jnp.bfloat16
MESH = pl.DeviceIdType.MESH

CORES, XS, YS, ZLO, ZHI = 2, 4, 8, 4, 2
ZS = ZLO * ZHI
T, D = 256, 1536
QUARTER = D // 4
LANES = 128
CHUNKS = QUARTER // LANES
WIDE = 4 * LANES
EDGE = 16
TILE = 16
ROWS = 6 * T * T // LANES
REGIONS = (32, 16)
HALF, PX, PY = ROWS // CORES, ROWS // (CORES * XS), ROWS // (CORES * XS * YS)


def far(v):
    return jnp.concatenate([v[:, 2 * LANES :], v[:, : 2 * LANES]], axis=1)


def near(v):
    a, b, c, d = (v[:, i * LANES : (i + 1) * LANES] for i in range(4))
    return jnp.concatenate([b, a, d, c], axis=1)


def mm(a, b):
    return jnp.dot(a, b, preferred_element_type=F32)


def mm_nt(a, b):
    return lax.dot_general(a, b, (((1,), (1,)), ((), ())), preferred_element_type=F32)


def kernel(
    tok_hbm, cot_hbm, taps_hbm, mixes_hbm, gain_ref,
    out_hbm, ag, e_out,
    tok, cot, halo, pad, conv, gf2, h, f2, t2, s2, gt, gs2, g1, fourth,
    gcpad, ggg, outb, edge_out, edges, wts, taps_ref, mixes_ref,
    m0, m12, m3, m45, m0t, m12t, m3t, m45t,
    grads, own_x, core_out, core_in, x_out, x_in, y_out, y_in, z_in,
    e_own, e_core, e_x, e_y, e_z,
    param_sem, in_send, in_recv, in_local, halo_send, halo_recv, edge_send, edge_recv,
    out_send, out_recv, out_local, core_send, core_recv, x_send, x_recv, y_send, y_recv,
    z_send, z_recv, gy_send, gy_recv, gx_send, gx_recv, gc_send, gc_recv,
    ec_sem, ex_send, ex_recv, ey_send, ey_recv, ez_send, ez_recv, eq_send, eq_recv,
):
    dp, k = lax.axis_index("dp"), lax.axis_index("seq")
    core, x, z_hi = lax.rem(dp, CORES), lax.rem(lax.div(dp, CORES), XS), lax.div(dp, CORES * XS)
    y, z_lo = lax.rem(k, YS), lax.div(k, YS)
    z = z_hi * ZLO + z_lo
    yb, yp = lax.rem(y, 2), lax.div(y, 2)
    zb, zp = lax.div(z_lo, 2), lax.rem(z_lo, 2)
    q = yb + 2 * zb

    def at(core_=core, x_=x, y_=y, z_=z):
        return (lax.div(z_, ZLO) * (XS * CORES) + x_ * CORES + core_, lax.rem(z_, ZLO) * YS + y_)

    def in_group(yp_, zp_, quarter):
        return (dp, (zp_ + 2 * lax.div(quarter, 2)) * YS + 2 * yp_ + lax.rem(quarter, 2))

    last_y, first_y = yp == YS // 2 - 1, yp == 0
    next_yp, next_zp = lax.rem(yp + 1, YS // 2), jnp.where(last_y, 1 - zp, zp)
    prev_yp, prev_zp = lax.rem(yp + YS // 2 - 1, YS // 2), jnp.where(first_y, 1 - zp, zp)
    next_flip = jnp.where(last_y, zp, 0)
    prev_flip = jnp.where(first_y, 1 - zp, 0)
    has_prev = 1.0 - prev_flip.astype(F32)
    has_next = 1.0 - next_flip.astype(F32)

    mates = [lax.rem(q + m, 4) for m in range(1, 4)]

    def rcopy(src, dst, send, recv, device):
        return pltpu.make_async_remote_copy(
            src_ref=src, dst_ref=dst, send_sem=send, recv_sem=recv, device_id=device, device_id_type=MESH
        )

    def lanes(quarter, c):
        return pl.ds(pl.multiple_of(quarter * QUARTER + c * LANES, LANES), LANES)

    params = [
        pltpu.make_async_copy(src, dst, param_sem.at[i])
        for i, (src, dst) in enumerate(((mixes_hbm, mixes_ref), (taps_hbm, taps_ref)))
    ]
    for copy in params:
        copy.start()

    barrier = pltpu.get_barrier_semaphore()
    others = [in_group(yp, zp, m) for m in mates]
    others += [in_group(next_yp, next_zp, m) for m in range(4)]
    others += [in_group(prev_yp, prev_zp, m) for m in range(4)]
    others += [at(core_=1 - core)]
    others += [at(x_=lax.rem(x + i, XS)) for i in range(1, XS)]
    others += [at(y_=lax.rem(y + i, YS)) for i in range(1, YS)]
    others += [at(z_=lax.rem(z + i, ZS)) for i in range(1, ZS)]
    for device in others:
        pl.semaphore_signal(barrier, inc=1, device_id=device, device_id_type=MESH)
    pl.semaphore_wait(barrier, len(others))

    halo_yp, halo_zp = jnp.where(yb == 1, next_yp, prev_yp), jnp.where(yb == 1, next_zp, prev_zp)
    halo_flip = jnp.where(yb == 1, next_flip, prev_flip)
    halo_half = lax.rem(zb + halo_flip, 2)
    halo_slot = (1 - yb) * 2 + halo_half
    halo_row = pl.multiple_of(yb * (T - EDGE), EDGE)
    halo_copies = [
        rcopy(
            tok_hbm.at[pl.ds(halo_row, EDGE), pl.ds(m * QUARTER, QUARTER)],
            halo.at[halo_slot],
            halo_send.at[m],
            halo_recv.at[halo_slot],
            in_group(halo_yp, halo_zp, m),
        )
        for m in range(4)
    ]
    for copy in halo_copies:
        copy.start()

    def inbound(c):
        copies = []
        for m in (1, 2, 0):
            for a in range(2):
                src, dst = ((tok_hbm, tok), (cot_hbm, cot))[a]
                copies.append(
                    rcopy(
                        src.at[:, lanes(mates[m], c)],
                        dst.at[c, q],
                        in_send.at[a, c, m],
                        in_recv.at[a, c, 2 - m],
                        in_group(yp, zp, mates[m]),
                    )
                )
        return copies

    def local(c):
        return [
            pltpu.make_async_copy(src.at[:, lanes(q, c)], dst.at[c, q], in_local.at[a, c])
            for a, (src, dst) in enumerate(((tok_hbm, tok), (cot_hbm, cot)))
        ]

    for c in range(CHUNKS):
        for copy in inbound(c) + local(c):
            copy.start()

    def transposed(v):
        return v.astype(F32).T.astype(BF16)

    for copy in params:
        copy.wait()
    m0[...] = mixes_ref[0]
    m12[:, :T], m12[:, T:] = mixes_ref[1], mixes_ref[2]
    m3[...] = mixes_ref[3]
    m45[:, :T], m45[:, T:] = mixes_ref[4], mixes_ref[5]
    m0t[...] = transposed(mixes_ref[0])
    m12t[:, :T], m12t[:, T:] = transposed(mixes_ref[1]), transposed(mixes_ref[2])
    m3t[...] = transposed(mixes_ref[3])
    m45t[:, :T], m45t[:, T:] = transposed(mixes_ref[4]), transposed(mixes_ref[5])
    wts[0:3, :] = taps_ref[...].astype(F32)
    for i in range(D // LANES):
        wts[3:4, i * LANES : (i + 1) * LANES] = gain_ref[i : i + 1, :]
    grads[...] = jnp.zeros_like(grads)
    e_own[...] = jnp.zeros_like(e_own)

    def weights(c):
        w = wts[:, lanes(q, c)]
        w = jnp.concatenate([w] * 4, axis=1)
        return [w[i : i + 1] for i in range(4)]

    def fill_edges(ref, prev, nxt):
        body = ref[8 : 16, :], ref[T : T + 8, :]
        first, last = body[0][0:1], body[1][7:8]
        ref[7:8, :] = jnp.concatenate([prev[0], last[:, :LANES], prev[1], last[:, 2 * LANES : 3 * LANES]], axis=1)
        ref[T + 8 : T + 9, :] = jnp.concatenate(
            [first[:, LANES : 2 * LANES], nxt[0], first[:, 3 * LANES :], nxt[1]], axis=1
        )

    def mask_edges(prev, nxt):
        return [prev[0] * has_prev, prev[1]], [nxt[0], nxt[1] * has_next]

    def tile_rows(i):
        return pl.ds(pl.multiple_of(i * TILE, TILE), TILE)

    def window(ref, i):
        w = ref[pl.ds(pl.multiple_of(i * TILE, TILE), TILE + 16), :]
        return w[7 : 7 + TILE], w[8 : 8 + TILE], w[9 : 9 + TILE]

    def edge_copies(c):
        copies = []
        for half in range(2):
            for side, (yp_, zp_, flip) in enumerate(((next_yp, next_zp, next_flip), (prev_yp, prev_zp, prev_flip))):
                slot = side * 2 + lax.rem(half + flip, 2)
                copies.append(
                    rcopy(
                        edge_out.at[c, side * 2 + half],
                        edges.at[c, slot],
                        edge_send.at[c, side * 2 + half],
                        edge_recv.at[c, slot],
                        in_group(yp_, zp_, q),
                    )
                )
        return copies

    def edge_wait(c):
        for slot in range(4):
            rcopy(
                edge_out.at[c, slot], edges.at[c, slot], edge_send.at[c, slot], edge_recv.at[c, slot],
                in_group(next_yp, next_zp, q),
            ).wait_recv()

    def wait_inbound(c):
        for a in range(2):
            dst = (tok, cot)[a]
            for m in range(3):
                rcopy(
                    dst.at[c, q], dst.at[c, mates[m]], in_send.at[a, c, m], in_recv.at[a, c, m],
                    in_group(yp, zp, mates[m]),
                ).wait_recv()
        for copy in local(c):
            copy.wait()

    def chain(c):
        for b in range(4):
            pad[8 : 8 + T, b * LANES : (b + 1) * LANES] = tok[c, b].astype(F32)
        chunk = pl.ds(pl.multiple_of(c * LANES, LANES), LANES)
        ends = [halo[s, :, chunk].astype(F32) for s in range(4)]
        fill_edges(
            pad, *mask_edges([ends[0][EDGE - 1 :], ends[1][EDGE - 1 :]], [ends[2][:1], ends[3][:1]])
        )
        w = weights(c)

        def before(i, carry):
            prev, cur, nxt = window(pad, i)
            rows = tile_rows(i)
            conv[rows, :] = (w[0] * prev + w[1] * cur + w[2] * nxt).astype(BF16)
            up = jnp.concatenate([cot[c, b, rows, :] for b in range(4)], axis=1).astype(F32)
            gate = w[3] * cur
            sig = 1.0 / (1.0 + jnp.exp(-gate))
            gf = (up * gate * sig).astype(BF16)
            gf2[rows, :] = gf
            gf2[pl.ds(pl.multiple_of(T + i * TILE, TILE), TILE), :] = near(gf)
            h[rows, :] = up * sig * (1.0 + gate * (1.0 - sig))
            return carry

        lax.fori_loop(0, T // TILE, before, 0)

        first = mm(m0[...], conv[...]).astype(BF16)
        f2[:T, :], f2[T:, :] = first, far(first)
        third_grad = mm(m45t[...], gf2[...]).astype(BF16)
        gt[...] = third_grad
        s2[...] = mm(m12[...], f2[...]).astype(BF16)
        second_grad = mm(m3t[...], gt[...]).astype(BF16)
        gs2[:T, :], gs2[T:, :] = second_grad, far(second_grad)
        third = mm(m3[...], s2[...]).astype(BF16)
        t2[:T, :], t2[T:, :] = third, near(third)
        g1[...] = mm(m12t[...], gs2[...]).astype(BF16)
        fourth[...] = mm(m45[...], t2[...])
        gc = mm(m0t[...], g1[...]).astype(BF16)
        gcpad[c, 8 : 8 + T, :] = gc.astype(F32)
        for half in range(2):
            odd = slice((2 * half + 1) * LANES, (2 * half + 2) * LANES)
            even = slice(2 * half * LANES, (2 * half + 1) * LANES)
            edge_out[c, half] = gc[T - EDGE :, odd]
            edge_out[c, 2 + half] = gc[:EDGE, even]
        for copy in edge_copies(c):
            copy.start()

        def add_grad(i, value):
            grads[2 * i * T : (2 * i + 1) * T, :] += value[:, :LANES]
            grads[(2 * i + 1) * T : (2 * i + 2) * T, :] += value[:, LANES:]

        add_grad(0, mm_nt(g1[...], conv[...]))
        add_grad(3, mm_nt(gt[...], s2[...]))
        both = mm_nt(gs2[:T, :], f2[...])
        add_grad(1, both[:, :T])
        add_grad(2, both[:, T:])
        both = mm_nt(gf2[:T, :], t2[...])
        add_grad(4, both[:, :T])
        add_grad(5, both[:, T:])

    def sums(c):
        w = weights(c)

        def after(i, carry):
            prev, cur, nxt = window(pad, i)
            rows = tile_rows(i)
            gg = h[rows, :] * fourth[rows, :]
            gc = gcpad[c, pl.ds(pl.multiple_of(8 + i * TILE, 8), TILE), :]
            ggg[c, rows, :] = gg * w[3]

            def fold(v):
                return v[:8] + v[8:]

            return tuple(
                have + fold(v) for have, v in zip(carry, (gc * prev, gc * cur, gc * nxt, gg * cur))
            )

        zero = jnp.zeros((8, WIDE), F32)
        totals = lax.fori_loop(0, T // TILE, after, (zero,) * 4)
        for j, total in enumerate(totals):
            row = jnp.sum(total, axis=0, keepdims=True)
            e_own[c, j : j + 1, :] = sum(row[:, b * LANES : (b + 1) * LANES] for b in range(4))

    def finish(c):
        edge_wait(c)
        ends = [edges[c, s].astype(F32) for s in range(4)]
        fill_edges(
            gcpad.at[c], *mask_edges([ends[0][EDGE - 1 :], ends[1][EDGE - 1 :]], [ends[2][:1], ends[3][:1]])
        )
        w = weights(c)

        def close(i, carry):
            prev, cur, nxt = window(gcpad.at[c], i)
            rows = tile_rows(i)
            out = (w[0] * nxt + w[1] * cur + w[2] * prev + ggg[c, rows, :]).astype(BF16)
            for b in range(4):
                outb[c, b, rows, :] = out[:, b * LANES : (b + 1) * LANES]
            return carry

        lax.fori_loop(0, T // TILE, close, 0)

    def outbound(c):
        return [
            rcopy(
                outb.at[c, mates[m]],
                out_hbm.at[:, lanes(q, c)],
                out_send.at[c, m],
                out_recv.at[c, 2 - m],
                in_group(yp, zp, mates[m]),
            )
            for m in (1, 2, 0)
        ]

    def out_own(c):
        return pltpu.make_async_copy(outb.at[c, q], out_hbm.at[:, lanes(q, c)], out_local.at[c])

    def send_out(c):
        for copy in outbound(c):
            copy.start()
        out_own(c).start()

    for slot in range(4):
        rcopy(
            tok_hbm.at[pl.ds(0, EDGE), pl.ds(0, QUARTER)], halo.at[slot], halo_send.at[slot], halo_recv.at[slot],
            in_group(next_yp, next_zp, q),
        ).wait_recv()

    def step(c, carry):
        wait_inbound(c)
        chain(c)

        @pl.when(c < CHUNKS - 1)
        def _():
            sums(c)

        @pl.when(c == CHUNKS - 2)
        def _():
            finish(0)

        return carry

    lax.fori_loop(0, CHUNKS, step, 0)

    sibling = at(core_=1 - core)
    x_mates = [lax.rem(x + i, XS) for i in range(1, XS)]
    y_mates = [lax.rem(y + i, YS) for i in range(1, YS)]
    z_mates = [lax.rem(z + i, ZS) for i in range(1, ZS)]

    def rows_of(start, size):
        return pl.ds(pl.multiple_of(start, EDGE), size)

    sent = list(halo_copies)

    def begin(copies):
        for copy in copies:
            copy.start()
        sent.extend(copies)
        return copies

    def slot_wait(ref, slot, send, recv):
        rcopy(ref.at[slot], ref.at[slot], send, recv, sibling).wait_recv()

    def offset(r):
        return CORES * XS * YS * sum(REGIONS[:r]) // CORES

    def sizes(r):
        return offset(r), YS * REGIONS[r], REGIONS[r]

    def core_stage(r):
        base, px, py = sizes(r)
        there = pl.ds(base, XS * px)
        core_out[there, :] = grads[rows_of((1 - core) * HALF + base, XS * px), :].astype(BF16)
        return begin([rcopy(core_out.at[there], core_in.at[there], core_send.at[r], core_recv.at[r], sibling)])

    def x_stage(r, copies):
        base, px, py = sizes(r)
        for copy in copies:
            copy.wait_recv()
        rows = pl.ds(base // XS, px)
        started = []
        for i, other in enumerate(x_mates):
            part = grads[rows_of(core * HALF + base + other * px, px), :]
            x_out[i, rows, :] = (part + core_in[rows_of(base + other * px, px), :].astype(F32)).astype(BF16)
            started += begin(
                [rcopy(x_out.at[i, rows], x_in.at[i, rows], x_send.at[r, i], x_recv.at[r, i], at(x_=other))]
            )
        part = grads[rows_of(core * HALF + base + x * px, px), :]
        own_x[rows, :] = part + core_in[rows_of(base + x * px, px), :].astype(F32)
        return started

    def y_stage(r, copies):
        base, px, py = sizes(r)
        for copy in copies:
            copy.wait_recv()
        rows = pl.ds(base // XS, px)
        own_x[rows, :] += sum(x_in[i, rows, :].astype(F32) for i in range(XS - 1))
        y_out[rows, :] = own_x[rows, :].astype(BF16)
        there = pl.ds(base // (XS * YS), py)
        return begin(
            [
                rcopy(
                    y_out.at[rows_of(base // XS + other * py, py)],
                    y_in.at[i, there],
                    y_send.at[r, i],
                    y_recv.at[r, i],
                    at(y_=other),
                )
                for i, other in enumerate(y_mates)
            ]
        )

    def z_stage(r, copies):
        base, px, py = sizes(r)
        for copy in copies:
            copy.wait_recv()
        rows = pl.ds(base // (XS * YS), py)
        total = own_x[rows_of(base // XS + y * py, py), :]
        total = total + sum(y_in[i, rows, :].astype(F32) for i in range(YS - 1))
        z_in[z, rows, :] = total.astype(BF16)
        return begin(
            [
                rcopy(z_in.at[z, rows], z_in.at[z, rows], z_send.at[r, i], z_recv.at[r, i], at(z_=other))
                for i, other in enumerate(z_mates)
            ]
        )

    def gather_y(r):
        base, px, py = sizes(r)
        rows = pl.ds(base // (XS * YS), py)
        for i in range(ZS - 1):
            there = z_in.at[lax.rem(z + ZS - 1 - i, ZS), rows]
            rcopy(there, there, z_send.at[r, i], z_recv.at[r, i], sibling).wait_recv()
        total = z_in[0, rows, :].astype(F32)
        for i in range(1, ZS):
            total = total + z_in[i, rows, :].astype(F32)
        own = rows_of(core * HALF + base + x * px + y * py, py)
        ag[own, :] = total.astype(BF16)
        begin(
            [
                rcopy(ag.at[own], ag.at[own], gy_send.at[r, i], gy_recv.at[r, i], at(y_=other))
                for i, other in enumerate(y_mates)
            ]
        )

    def gather_x(r):
        base, px, py = sizes(r)
        for i in range(YS - 1):
            there = ag.at[rows_of(core * HALF + base + x * px + lax.rem(y + YS - 1 - i, YS) * py, py)]
            rcopy(there, there, gy_send.at[r, i], gy_recv.at[r, i], sibling).wait_recv()
        mine = ag.at[rows_of(core * HALF + base + x * px, px)]
        begin(
            [
                rcopy(mine, mine, gx_send.at[r, i], gx_recv.at[r, i], at(x_=other))
                for i, other in enumerate(x_mates)
            ]
            + [rcopy(mine, mine, gc_send.at[r, 0], gc_recv.at[r, 0], sibling)]
        )

    def gather_core(r):
        base, px, py = sizes(r)
        for i in range(XS - 1):
            there = ag.at[rows_of(core * HALF + base + lax.rem(x + XS - 1 - i, XS) * px, px)]
            rcopy(there, there, gx_send.at[r, i], gx_recv.at[r, i], sibling).wait_recv()
            begin([rcopy(there, there, gc_send.at[r, i + 1], gc_recv.at[r, i + 1], sibling)])

    def gather_end(r):
        base, px, py = sizes(r)
        for i in range(XS):
            there = ag.at[rows_of((1 - core) * HALF + base + lax.rem(x + XS - i, XS) * px, px)]
            rcopy(there, there, gc_send.at[r, i], gc_recv.at[r, i], sibling).wait_recv()

    regions = range(len(REGIONS))
    flights = [core_stage(r) for r in regions]
    send_out(0)
    sums(CHUNKS - 1)
    e_core_copy = begin([rcopy(e_own, e_core, ec_sem.at[0], ec_sem.at[1], sibling)])[0]
    flights = [x_stage(r, flights[r]) for r in regions]
    for past in range(1, CHUNKS - 1):
        finish(past)
        send_out(past)
    e_core_copy.wait_recv()
    e_x[x] = e_own[...] + e_core[...]
    begin(
        [rcopy(e_x.at[x], e_x.at[x], ex_send.at[i], ex_recv.at[i], at(x_=other)) for i, other in enumerate(x_mates)]
    )
    finish(CHUNKS - 1)
    send_out(CHUNKS - 1)
    flights = [y_stage(r, flights[r]) for r in regions]

    for i in range(XS - 1):
        slot_wait(e_x, lax.rem(x + XS - 1 - i, XS), ex_send.at[i], ex_recv.at[i])
    e_y[yp] = e_x[0] + e_x[1] + e_x[2] + e_x[3]
    begin(
        [
            rcopy(e_y.at[yp], e_y.at[yp], ey_send.at[i], ey_recv.at[i], at(y_=lax.rem(y + 2 * (i + 1), YS)))
            for i in range(3)
        ]
    )
    for r in regions:
        z_stage(r, flights[r])

    for i in range(3):
        slot_wait(e_y, lax.rem(yp + 3 - i, 4), ey_send.at[i], ey_recv.at[i])
    ez_me = z_hi * 2 + zp
    e_z[ez_me] = e_y[0] + e_y[1] + e_y[2] + e_y[3]

    def ez_device(slot):
        return at(z_=lax.div(slot, 2) * ZLO + 2 * zb + lax.rem(slot, 2))

    begin(
        [
            rcopy(e_z.at[ez_me], e_z.at[ez_me], ez_send.at[i], ez_recv.at[i], ez_device(lax.rem(ez_me + i + 1, 4)))
            for i in range(3)
        ]
    )
    for r in regions:
        gather_y(r)

    for i in range(3):
        slot_wait(e_z, lax.rem(ez_me + 3 - i, 4), ez_send.at[i], ez_recv.at[i])
    e_out[q] = e_z[0] + e_z[1] + e_z[2] + e_z[3]
    begin(
        [
            rcopy(e_out.at[q], e_out.at[q], eq_send.at[i], eq_recv.at[i], in_group(yp, zp, mates[i]))
            for i in range(3)
        ]
    )
    for r in regions:
        gather_x(r)
    for r in regions:
        gather_core(r)

    for i in range(3):
        slot_wait(e_out, mates[2 - i], eq_send.at[i], eq_recv.at[i])
    for c in range(CHUNKS):
        for m in range(3):
            rcopy(
                outb.at[c, mates[m]], out_hbm.at[:, lanes(mates[m], c)], out_send.at[c, m], out_recv.at[c, m], sibling
            ).wait_recv()
        out_own(c).wait()
    for r in regions:
        gather_end(r)
    for c in range(CHUNKS):
        sent += inbound(c) + edge_copies(c) + outbound(c)
    for copy in sent:
        copy.wait_send()


def closing_kernel(grad_ref, ag_ref, small_ref, grad_out, mixes_out, taps_out, gain_out, *, mix_scale, tok_scale):
    grad_out[...] = grad_ref[...]
    for m in range(mixes_out.shape[0]):
        for side in range(2):
            part = ag_ref[(2 * m + side) * T : (2 * m + side + 1) * T, :].astype(F32)
            mixes_out[m, :, side * LANES : (side + 1) * LANES] = part * mix_scale
    for i in range(D // LANES):
        part = small_ref[i // CHUNKS, i % CHUNKS] * tok_scale
        taps_out[:, i * LANES : (i + 1) * LANES] = part[:3]
        gain_out[i : i + 1, :] = part[3:4]


def local(tokens, cotangent, conv_taps, block_mixes, gate_gain):
    slabs = lax.axis_size("dp")
    tok_scale = 1.0 / math.sqrt(slabs * lax.axis_size("seq") * T)
    mix_scale = 1.0 / math.sqrt(slabs * lax.axis_size("seq") * D)
    small = (CHUNKS, 8, LANES)
    dma = pltpu.SemaphoreType.DMA
    wide = (T, WIDE)
    scratch = [
        *[pltpu.VMEM((CHUNKS, 4, T, LANES), BF16)] * 2,
        pltpu.VMEM((4, EDGE, QUARTER), BF16),
        pltpu.VMEM((T + 16, WIDE), F32),
        pltpu.VMEM(wide, BF16),
        pltpu.VMEM((2 * T, WIDE), BF16),
        pltpu.VMEM(wide, F32),
        pltpu.VMEM((2 * T, WIDE), BF16),
        pltpu.VMEM((2 * T, WIDE), BF16),
        pltpu.VMEM(wide, BF16),
        pltpu.VMEM(wide, BF16),
        pltpu.VMEM((2 * T, WIDE), BF16),
        pltpu.VMEM(wide, BF16),
        pltpu.VMEM(wide, F32),
        pltpu.VMEM((CHUNKS, T + 16, WIDE), F32),
        pltpu.VMEM((CHUNKS, T, WIDE), F32),
        pltpu.VMEM((CHUNKS, 4, T, LANES), BF16),
        *[pltpu.VMEM((CHUNKS, 4, EDGE, LANES), BF16)] * 2,
        pltpu.VMEM((8, D), F32),
        pltpu.VMEM((3, D), BF16),
        pltpu.VMEM((6, T, T), BF16),
        *[pltpu.VMEM((T, n * T), BF16) for n in (1, 2, 1, 2, 1, 2, 1, 2)],
        pltpu.VMEM((ROWS, LANES), F32),
        pltpu.VMEM((PX, LANES), F32),
        *[pltpu.VMEM((HALF, LANES), BF16)] * 2,
        *[pltpu.VMEM((XS - 1, PX, LANES), BF16)] * 2,
        pltpu.VMEM((PX, LANES), BF16),
        pltpu.VMEM((YS - 1, PY, LANES), BF16),
        pltpu.VMEM((ZS, PY, LANES), BF16),
        *[pltpu.VMEM(small, F32)] * 2,
        *[pltpu.VMEM((4, *small), F32)] * 3,
        dma((2,)),
        *[dma((2, CHUNKS, 3))] * 2, dma((2, CHUNKS)),
        *[dma((4,))] * 2,
        *[dma((CHUNKS, 4))] * 2,
        *[dma((CHUNKS, 3))] * 2, dma((CHUNKS,)),
        *[dma((len(REGIONS),))] * 2,
        *[dma((len(REGIONS), XS - 1))] * 2,
        *[dma((len(REGIONS), YS - 1))] * 2,
        *[dma((len(REGIONS), ZS - 1))] * 2,
        *[dma((len(REGIONS), YS - 1))] * 2,
        *[dma((len(REGIONS), XS - 1))] * 2,
        *[dma((len(REGIONS), XS))] * 2,
        dma((2,)),
        *[dma((3,))] * 8,
    ]
    vmem, hbm = pl.BlockSpec(memory_space=pltpu.VMEM), pl.BlockSpec(memory_space=pltpu.HBM)
    flops = 18 * 2 * T * T * D
    input_grad, mixes, small_sums = pl.pallas_call(
        kernel,
        out_shape=(
            jax.ShapeDtypeStruct((T, D), BF16),
            jax.ShapeDtypeStruct((ROWS, LANES), BF16),
            jax.ShapeDtypeStruct((4, *small), F32),
        ),
        in_specs=[hbm, hbm, hbm, hbm, vmem],
        out_specs=(pl.BlockSpec(memory_space=pl.ANY), vmem, vmem),
        scratch_shapes=scratch,
        compiler_params=pltpu.CompilerParams(
            collective_id=0, has_side_effects=True, vmem_limit_bytes=56 * 1024 * 1024
        ),
        cost_estimate=pl.CostEstimate(flops=flops, bytes_accessed=6 * T * D, transcendentals=T * D),
    )(tokens[0], cotangent[0], conv_taps, block_mixes, gate_gain.reshape(D // LANES, LANES))
    steps = 3
    fixed = lambda shape: pl.BlockSpec(shape, lambda i: (0,) * len(shape))
    input_grad, mixes_grad, taps_grad, gain_grad = pl.pallas_call(
        functools.partial(closing_kernel, mix_scale=mix_scale, tok_scale=tok_scale),
        grid=(steps,),
        out_shape=(
            jax.ShapeDtypeStruct((T, D), BF16),
            jax.ShapeDtypeStruct((6, T, T), F32),
            jax.ShapeDtypeStruct((3, D), F32),
            jax.ShapeDtypeStruct((D // LANES, LANES), F32),
        ),
        in_specs=[
            pl.BlockSpec((T, D // steps), lambda i: (0, i)),
            pl.BlockSpec((ROWS // steps, LANES), lambda i: (i, 0)),
            fixed((4, *small)),
        ],
        out_specs=(
            pl.BlockSpec((T, D // steps), lambda i: (0, i)),
            pl.BlockSpec((6 // steps, T, T), lambda i: (i, 0, 0)),
            fixed((3, D)),
            fixed((D // LANES, LANES)),
        ),
    )(input_grad, mixes, small_sums)
    return input_grad[None], mixes_grad, taps_grad, gain_grad.reshape(D)


def solution(mesh):
    placed = (P("dp", "seq", None), P("dp", "seq", None), P(), P(), P())
    return jax.shard_map(
        local,
        mesh=mesh,
        in_specs=placed,
        out_specs=(P("dp", "seq", None), P(), P(), P()),
        check_vma=False,
    )
```

```python
import functools
import math

import jax
import jax.numpy as jnp
from jax import lax
from jax.experimental import pallas as pl
from jax.experimental.pallas import tpu as pltpu
from jax.sharding import PartitionSpec as P

F32, BF16 = jnp.float32, jnp.bfloat16
MESH = pl.DeviceIdType.MESH

CORES, XS, YS, ZLO, ZHI = 2, 4, 8, 4, 2
ZS = ZLO * ZHI
T, D = 256, 1536
QUARTER = D // 4
LANES = 128
CHUNKS = QUARTER // LANES
WIDE = 4 * LANES
EDGE = 16
TILE = 16
ROWS = 6 * T * T // LANES
REGIONS = (32, 16)
HALF, PX, PY = ROWS // CORES, ROWS // (CORES * XS), ROWS // (CORES * XS * YS)


def far(v):
    return jnp.concatenate([v[:, 2 * LANES :], v[:, : 2 * LANES]], axis=1)


def near(v):
    a, b, c, d = (v[:, i * LANES : (i + 1) * LANES] for i in range(4))
    return jnp.concatenate([b, a, d, c], axis=1)


def mm(a, b):
    return jnp.dot(a, b, preferred_element_type=F32)


def mm_nt(a, b):
    return lax.dot_general(a, b, (((1,), (1,)), ((), ())), preferred_element_type=F32)


def kernel(
    tok_hbm, cot_hbm, taps_hbm, mixes_hbm, gain_ref,
    out_hbm, ag, e_out,
    tok, cot, halo, pad, conv, gf2, h, f2, t2, s2, gt, gs2, g1, fourth,
    gcpad, ggg, outb, edge_out, edges, wts, taps_ref, mixes_ref,
    m0, m12, m3, m45, m0t, m12t, m3t, m45t,
    grads, own_x, core_out, core_in, x_out, x_in, y_out, y_in, z_in,
    e_own, e_core, e_x, e_y, e_z,
    param_sem, in_send, in_recv, in_local, halo_send, halo_recv, edge_send, edge_recv,
    out_send, out_recv, out_local, core_send, core_recv, x_send, x_recv, y_send, y_recv,
    z_send, z_recv, gy_send, gy_recv, gx_send, gx_recv, gc_send, gc_recv,
    ec_sem, ex_send, ex_recv, ey_send, ey_recv, ez_send, ez_recv, eq_send, eq_recv,
):
    dp, k = lax.axis_index("dp"), lax.axis_index("seq")
    core, x, z_hi = lax.rem(dp, CORES), lax.rem(lax.div(dp, CORES), XS), lax.div(dp, CORES * XS)
    y, z_lo = lax.rem(k, YS), lax.div(k, YS)
    z = z_hi * ZLO + z_lo
    yb, yp = lax.rem(y, 2), lax.div(y, 2)
    zb, zp = lax.div(z_lo, 2), lax.rem(z_lo, 2)
    q = yb + 2 * zb

    def at(core_=core, x_=x, y_=y, z_=z):
        return (lax.div(z_, ZLO) * (XS * CORES) + x_ * CORES + core_, lax.rem(z_, ZLO) * YS + y_)

    def in_group(yp_, zp_, quarter):
        return (dp, (zp_ + 2 * lax.div(quarter, 2)) * YS + 2 * yp_ + lax.rem(quarter, 2))

    last_y, first_y = yp == YS // 2 - 1, yp == 0
    next_yp, next_zp = lax.rem(yp + 1, YS // 2), jnp.where(last_y, 1 - zp, zp)
    prev_yp, prev_zp = lax.rem(yp + YS // 2 - 1, YS // 2), jnp.where(first_y, 1 - zp, zp)
    next_flip = jnp.where(last_y, zp, 0)
    prev_flip = jnp.where(first_y, 1 - zp, 0)
    has_prev = 1.0 - prev_flip.astype(F32)
    has_next = 1.0 - next_flip.astype(F32)

    mates = [lax.rem(q + m, 4) for m in range(1, 4)]

    def rcopy(src, dst, send, recv, device):
        return pltpu.make_async_remote_copy(
            src_ref=src, dst_ref=dst, send_sem=send, recv_sem=recv, device_id=device, device_id_type=MESH
        )

    def lanes(quarter, c):
        return pl.ds(pl.multiple_of(quarter * QUARTER + c * LANES, LANES), LANES)

    params = [
        pltpu.make_async_copy(src, dst, param_sem.at[i])
        for i, (src, dst) in enumerate(((mixes_hbm, mixes_ref), (taps_hbm, taps_ref)))
    ]
    for copy in params:
        copy.start()

    barrier = pltpu.get_barrier_semaphore()
    others = [in_group(yp, zp, m) for m in mates]
    others += [in_group(next_yp, next_zp, m) for m in range(4)]
    others += [in_group(prev_yp, prev_zp, m) for m in range(4)]
    others += [at(core_=1 - core)]
    others += [at(x_=lax.rem(x + i, XS)) for i in range(1, XS)]
    others += [at(y_=lax.rem(y + i, YS)) for i in range(1, YS)]
    others += [at(z_=lax.rem(z + i, ZS)) for i in range(1, ZS)]
    for device in others:
        pl.semaphore_signal(barrier, inc=1, device_id=device, device_id_type=MESH)
    pl.semaphore_wait(barrier, len(others))

    halo_yp, halo_zp = jnp.where(yb == 1, next_yp, prev_yp), jnp.where(yb == 1, next_zp, prev_zp)
    halo_flip = jnp.where(yb == 1, next_flip, prev_flip)
    halo_half = lax.rem(zb + halo_flip, 2)
    halo_slot = (1 - yb) * 2 + halo_half
    halo_row = pl.multiple_of(yb * (T - EDGE), EDGE)
    halo_copies = [
        rcopy(
            tok_hbm.at[pl.ds(halo_row, EDGE), pl.ds(m * QUARTER, QUARTER)],
            halo.at[halo_slot],
            halo_send.at[m],
            halo_recv.at[halo_slot],
            in_group(halo_yp, halo_zp, m),
        )
        for m in range(4)
    ]

    def inbound(c):
        copies = []
        for m in (1, 2, 0):
            for a in range(2):
                src, dst = ((tok_hbm, tok), (cot_hbm, cot))[a]
                copies.append(
                    rcopy(
                        src.at[:, lanes(mates[m], c)],
                        dst.at[c, q],
                        in_send.at[a, c, m],
                        in_recv.at[a, c, 2 - m],
                        in_group(yp, zp, mates[m]),
                    )
                )
        return copies

    def local(c):
        return [
            pltpu.make_async_copy(src.at[:, lanes(q, c)], dst.at[c, q], in_local.at[a, c])
            for a, (src, dst) in enumerate(((tok_hbm, tok), (cot_hbm, cot)))
        ]

    for c in range(CHUNKS):
        for copy in inbound(c) + local(c) + (halo_copies if c == 0 else []):
            copy.start()

    def transposed(v):
        return v.astype(F32).T.astype(BF16)

    for copy in params:
        copy.wait()
    m0[...] = mixes_ref[0]
    m12[:, :T], m12[:, T:] = mixes_ref[1], mixes_ref[2]
    m3[...] = mixes_ref[3]
    m45[:, :T], m45[:, T:] = mixes_ref[4], mixes_ref[5]
    m0t[...] = transposed(mixes_ref[0])
    m12t[:, :T], m12t[:, T:] = transposed(mixes_ref[1]), transposed(mixes_ref[2])
    m3t[...] = transposed(mixes_ref[3])
    m45t[:, :T], m45t[:, T:] = transposed(mixes_ref[4]), transposed(mixes_ref[5])
    wts[0:3, :] = taps_ref[...].astype(F32)
    for i in range(D // LANES):
        wts[3:4, i * LANES : (i + 1) * LANES] = gain_ref[i : i + 1, :]
    grads[...] = jnp.zeros_like(grads)
    e_own[...] = jnp.zeros_like(e_own)

    def weights(c):
        w = wts[:, lanes(q, c)]
        w = jnp.concatenate([w] * 4, axis=1)
        return [w[i : i + 1] for i in range(4)]

    def fill_edges(ref, prev, nxt):
        body = ref[8 : 16, :], ref[T : T + 8, :]
        first, last = body[0][0:1], body[1][7:8]
        ref[7:8, :] = jnp.concatenate([prev[0], last[:, :LANES], prev[1], last[:, 2 * LANES : 3 * LANES]], axis=1)
        ref[T + 8 : T + 9, :] = jnp.concatenate(
            [first[:, LANES : 2 * LANES], nxt[0], first[:, 3 * LANES :], nxt[1]], axis=1
        )

    def mask_edges(prev, nxt):
        return [prev[0] * has_prev, prev[1]], [nxt[0], nxt[1] * has_next]

    def tile_rows(i):
        return pl.ds(pl.multiple_of(i * TILE, TILE), TILE)

    def window(ref, i):
        w = ref[pl.ds(pl.multiple_of(i * TILE, TILE), TILE + 16), :]
        return w[7 : 7 + TILE], w[8 : 8 + TILE], w[9 : 9 + TILE]

    def edge_copies(c):
        copies = []
        for half in range(2):
            for side, (yp_, zp_, flip) in enumerate(((next_yp, next_zp, next_flip), (prev_yp, prev_zp, prev_flip))):
                slot = side * 2 + lax.rem(half + flip, 2)
                copies.append(
                    rcopy(
                        edge_out.at[c, side * 2 + half],
                        edges.at[c, slot],
                        edge_send.at[c, side * 2 + half],
                        edge_recv.at[c, slot],
                        in_group(yp_, zp_, q),
                    )
                )
        return copies

    def edge_wait(c):
        for slot in range(4):
            rcopy(
                edge_out.at[c, slot], edges.at[c, slot], edge_send.at[c, slot], edge_recv.at[c, slot],
                in_group(next_yp, next_zp, q),
            ).wait_recv()

    def wait_inbound(c):
        for a in range(2):
            dst = (tok, cot)[a]
            for m in range(3):
                rcopy(
                    dst.at[c, q], dst.at[c, mates[m]], in_send.at[a, c, m], in_recv.at[a, c, m],
                    in_group(yp, zp, mates[m]),
                ).wait_recv()
        for copy in local(c):
            copy.wait()

    def chain(c):
        for b in range(4):
            pad[c, 8 : 8 + T, b * LANES : (b + 1) * LANES] = tok[c, b].astype(F32)
        chunk = pl.ds(pl.multiple_of(c * LANES, LANES), LANES)
        ends = [halo[s, :, chunk].astype(F32) for s in range(4)]
        fill_edges(
            pad.at[c], *mask_edges([ends[0][EDGE - 1 :], ends[1][EDGE - 1 :]], [ends[2][:1], ends[3][:1]])
        )
        w = weights(c)

        def before(i, carry):
            prev, cur, nxt = window(pad.at[c], i)
            rows = tile_rows(i)
            conv[rows, :] = (w[0] * prev + w[1] * cur + w[2] * nxt).astype(BF16)
            up = jnp.concatenate([cot[c, b, rows, :] for b in range(4)], axis=1).astype(F32)
            gate = w[3] * cur
            sig = 1.0 / (1.0 + jnp.exp(-gate))
            gf = (up * gate * sig).astype(BF16)
            gf2[rows, :] = gf
            gf2[pl.ds(pl.multiple_of(T + i * TILE, TILE), TILE), :] = near(gf)
            h[c, rows, :] = up * sig * (1.0 + gate * (1.0 - sig))
            return carry

        lax.fori_loop(0, T // TILE, before, 0)

        first = mm(m0[...], conv[...]).astype(BF16)
        f2[:T, :], f2[T:, :] = first, far(first)
        third_grad = mm(m45t[...], gf2[...]).astype(BF16)
        gt[...] = third_grad
        s2[...] = mm(m12[...], f2[...]).astype(BF16)
        second_grad = mm(m3t[...], gt[...]).astype(BF16)
        gs2[:T, :], gs2[T:, :] = second_grad, far(second_grad)
        third = mm(m3[...], s2[...]).astype(BF16)
        t2[:T, :], t2[T:, :] = third, near(third)
        g1[...] = mm(m12t[...], gs2[...]).astype(BF16)
        fourth[c] = mm(m45[...], t2[...])
        gc = mm(m0t[...], g1[...]).astype(BF16)
        gcpad[c, 8 : 8 + T, :] = gc.astype(F32)
        for half in range(2):
            odd = slice((2 * half + 1) * LANES, (2 * half + 2) * LANES)
            even = slice(2 * half * LANES, (2 * half + 1) * LANES)
            edge_out[c, half] = gc[T - EDGE :, odd]
            edge_out[c, 2 + half] = gc[:EDGE, even]
        for copy in edge_copies(c):
            copy.start()

        def add_grad(i, value):
            grads[2 * i * T : (2 * i + 1) * T, :] += value[:, :LANES]
            grads[(2 * i + 1) * T : (2 * i + 2) * T, :] += value[:, LANES:]

        add_grad(0, mm_nt(g1[...], conv[...]))
        add_grad(3, mm_nt(gt[...], s2[...]))
        both = mm_nt(gs2[:T, :], f2[...])
        add_grad(1, both[:, :T])
        add_grad(2, both[:, T:])
        both = mm_nt(gf2[:T, :], t2[...])
        add_grad(4, both[:, :T])
        add_grad(5, both[:, T:])

    def sums(c):
        w = weights(c)

        def after(i, carry):
            prev, cur, nxt = window(pad.at[c], i)
            rows = tile_rows(i)
            gg = h[c, rows, :] * fourth[c, rows, :]
            gc = gcpad[c, pl.ds(pl.multiple_of(8 + i * TILE, 8), TILE), :]
            ggg[c, rows, :] = gg * w[3]

            def fold(v):
                return v[:8] + v[8:]

            return tuple(
                have + fold(v) for have, v in zip(carry, (gc * prev, gc * cur, gc * nxt, gg * cur))
            )

        zero = jnp.zeros((8, WIDE), F32)
        totals = lax.fori_loop(0, T // TILE, after, (zero,) * 4)
        for j, total in enumerate(totals):
            row = jnp.sum(total, axis=0, keepdims=True)
            e_own[c, j : j + 1, :] = sum(row[:, b * LANES : (b + 1) * LANES] for b in range(4))

    def finish(c):
        edge_wait(c)
        ends = [edges[c, s].astype(F32) for s in range(4)]
        fill_edges(
            gcpad.at[c], *mask_edges([ends[0][EDGE - 1 :], ends[1][EDGE - 1 :]], [ends[2][:1], ends[3][:1]])
        )
        w = weights(c)

        def close(i, carry):
            prev, cur, nxt = window(gcpad.at[c], i)
            rows = tile_rows(i)
            out = (w[0] * nxt + w[1] * cur + w[2] * prev + ggg[c, rows, :]).astype(BF16)
            for b in range(4):
                outb[c, b, rows, :] = out[:, b * LANES : (b + 1) * LANES]
            return carry

        lax.fori_loop(0, T // TILE, close, 0)

    def outbound(c):
        return [
            rcopy(
                outb.at[c, mates[m]],
                out_hbm.at[:, lanes(q, c)],
                out_send.at[c, m],
                out_recv.at[c, 2 - m],
                in_group(yp, zp, mates[m]),
            )
            for m in (1, 2, 0)
        ]

    def out_own(c):
        return pltpu.make_async_copy(outb.at[c, q], out_hbm.at[:, lanes(q, c)], out_local.at[c])

    def send_out(c):
        for copy in outbound(c):
            copy.start()
        out_own(c).start()

    for slot in range(4):
        rcopy(
            tok_hbm.at[pl.ds(0, EDGE), pl.ds(0, QUARTER)], halo.at[slot], halo_send.at[slot], halo_recv.at[slot],
            in_group(next_yp, next_zp, q),
        ).wait_recv()

    def step(c, carry):
        wait_inbound(c)
        chain(c)

        return carry

    lax.fori_loop(0, CHUNKS, step, 0)

    sibling = at(core_=1 - core)
    x_mates = [lax.rem(x + i, XS) for i in range(1, XS)]
    y_mates = [lax.rem(y + i, YS) for i in range(1, YS)]
    z_mates = [lax.rem(z + i, ZS) for i in range(1, ZS)]

    def rows_of(start, size):
        return pl.ds(pl.multiple_of(start, EDGE), size)

    sent = list(halo_copies)

    def begin(copies):
        for copy in copies:
            copy.start()
        sent.extend(copies)
        return copies

    def slot_wait(ref, slot, send, recv):
        rcopy(ref.at[slot], ref.at[slot], send, recv, sibling).wait_recv()

    def offset(r):
        return CORES * XS * YS * sum(REGIONS[:r]) // CORES

    def sizes(r):
        return offset(r), YS * REGIONS[r], REGIONS[r]

    def core_stage(r):
        base, px, py = sizes(r)
        there = pl.ds(base, XS * px)
        core_out[there, :] = grads[rows_of((1 - core) * HALF + base, XS * px), :].astype(BF16)
        return begin([rcopy(core_out.at[there], core_in.at[there], core_send.at[r], core_recv.at[r], sibling)])

    def x_stage(r, copies):
        base, px, py = sizes(r)
        for copy in copies:
            copy.wait_recv()
        rows = pl.ds(base // XS, px)
        started = []
        for i, other in enumerate(x_mates):
            part = grads[rows_of(core * HALF + base + other * px, px), :]
            x_out[i, rows, :] = (part + core_in[rows_of(base + other * px, px), :].astype(F32)).astype(BF16)
            started += begin(
                [rcopy(x_out.at[i, rows], x_in.at[i, rows], x_send.at[r, i], x_recv.at[r, i], at(x_=other))]
            )
        part = grads[rows_of(core * HALF + base + x * px, px), :]
        own_x[rows, :] = part + core_in[rows_of(base + x * px, px), :].astype(F32)
        return started

    def y_stage(r, copies):
        base, px, py = sizes(r)
        for copy in copies:
            copy.wait_recv()
        rows = pl.ds(base // XS, px)
        own_x[rows, :] += sum(x_in[i, rows, :].astype(F32) for i in range(XS - 1))
        y_out[rows, :] = own_x[rows, :].astype(BF16)
        there = pl.ds(base // (XS * YS), py)
        return begin(
            [
                rcopy(
                    y_out.at[rows_of(base // XS + other * py, py)],
                    y_in.at[i, there],
                    y_send.at[r, i],
                    y_recv.at[r, i],
                    at(y_=other),
                )
                for i, other in enumerate(y_mates)
            ]
        )

    def z_stage(r, copies):
        base, px, py = sizes(r)
        for copy in copies:
            copy.wait_recv()
        rows = pl.ds(base // (XS * YS), py)
        total = own_x[rows_of(base // XS + y * py, py), :]
        total = total + sum(y_in[i, rows, :].astype(F32) for i in range(YS - 1))
        z_in[z, rows, :] = total.astype(BF16)
        return begin(
            [
                rcopy(z_in.at[z, rows], z_in.at[z, rows], z_send.at[r, i], z_recv.at[r, i], at(z_=other))
                for i, other in enumerate(z_mates)
            ]
        )

    def gather_y(r):
        base, px, py = sizes(r)
        rows = pl.ds(base // (XS * YS), py)
        for i in range(ZS - 1):
            there = z_in.at[lax.rem(z + ZS - 1 - i, ZS), rows]
            rcopy(there, there, z_send.at[r, i], z_recv.at[r, i], sibling).wait_recv()
        total = z_in[0, rows, :].astype(F32)
        for i in range(1, ZS):
            total = total + z_in[i, rows, :].astype(F32)
        own = rows_of(core * HALF + base + x * px + y * py, py)
        ag[own, :] = total.astype(BF16)
        begin(
            [
                rcopy(ag.at[own], ag.at[own], gy_send.at[r, i], gy_recv.at[r, i], at(y_=other))
                for i, other in enumerate(y_mates)
            ]
        )

    def gather_x(r):
        base, px, py = sizes(r)
        for i in range(YS - 1):
            there = ag.at[rows_of(core * HALF + base + x * px + lax.rem(y + YS - 1 - i, YS) * py, py)]
            rcopy(there, there, gy_send.at[r, i], gy_recv.at[r, i], sibling).wait_recv()
        mine = ag.at[rows_of(core * HALF + base + x * px, px)]
        begin(
            [
                rcopy(mine, mine, gx_send.at[r, i], gx_recv.at[r, i], at(x_=other))
                for i, other in enumerate(x_mates)
            ]
            + [rcopy(mine, mine, gc_send.at[r, 0], gc_recv.at[r, 0], sibling)]
        )

    def gather_core(r):
        base, px, py = sizes(r)
        for i in range(XS - 1):
            there = ag.at[rows_of(core * HALF + base + lax.rem(x + XS - 1 - i, XS) * px, px)]
            rcopy(there, there, gx_send.at[r, i], gx_recv.at[r, i], sibling).wait_recv()
            begin([rcopy(there, there, gc_send.at[r, i + 1], gc_recv.at[r, i + 1], sibling)])

    def gather_end(r):
        base, px, py = sizes(r)
        for i in range(XS):
            there = ag.at[rows_of((1 - core) * HALF + base + lax.rem(x + XS - i, XS) * px, px)]
            rcopy(there, there, gc_send.at[r, i], gc_recv.at[r, i], sibling).wait_recv()

    regions = range(len(REGIONS))
    flights = [core_stage(r) for r in regions]
    for c in range(CHUNKS):
        sums(c)
    e_core_copy = begin([rcopy(e_own, e_core, ec_sem.at[0], ec_sem.at[1], sibling)])[0]
    flights = [x_stage(r, flights[r]) for r in regions]
    for past in range(CHUNKS - 1):
        finish(past)
        send_out(past)
    e_core_copy.wait_recv()
    e_x[x] = e_own[...] + e_core[...]
    begin(
        [rcopy(e_x.at[x], e_x.at[x], ex_send.at[i], ex_recv.at[i], at(x_=other)) for i, other in enumerate(x_mates)]
    )
    finish(CHUNKS - 1)
    flights = [y_stage(r, flights[r]) for r in regions]

    for i in range(XS - 1):
        slot_wait(e_x, lax.rem(x + XS - 1 - i, XS), ex_send.at[i], ex_recv.at[i])
    e_y[yp] = e_x[0] + e_x[1] + e_x[2] + e_x[3]
    begin(
        [
            rcopy(e_y.at[yp], e_y.at[yp], ey_send.at[i], ey_recv.at[i], at(y_=lax.rem(y + 2 * (i + 1), YS)))
            for i in range(3)
        ]
    )
    for r in regions:
        z_stage(r, flights[r])
    send_out(CHUNKS - 1)

    for i in range(3):
        slot_wait(e_y, lax.rem(yp + 3 - i, 4), ey_send.at[i], ey_recv.at[i])
    ez_me = z_hi * 2 + zp
    e_z[ez_me] = e_y[0] + e_y[1] + e_y[2] + e_y[3]

    def ez_device(slot):
        return at(z_=lax.div(slot, 2) * ZLO + 2 * zb + lax.rem(slot, 2))

    begin(
        [
            rcopy(e_z.at[ez_me], e_z.at[ez_me], ez_send.at[i], ez_recv.at[i], ez_device(lax.rem(ez_me + i + 1, 4)))
            for i in range(3)
        ]
    )
    for r in regions:
        gather_y(r)

    for i in range(3):
        slot_wait(e_z, lax.rem(ez_me + 3 - i, 4), ez_send.at[i], ez_recv.at[i])
    e_out[q] = e_z[0] + e_z[1] + e_z[2] + e_z[3]
    begin(
        [
            rcopy(e_out.at[q], e_out.at[q], eq_send.at[i], eq_recv.at[i], in_group(yp, zp, mates[i]))
            for i in range(3)
        ]
    )
    for r in regions:
        gather_x(r)
    for r in regions:
        gather_core(r)

    for i in range(3):
        slot_wait(e_out, mates[2 - i], eq_send.at[i], eq_recv.at[i])
    for c in range(CHUNKS):
        for m in range(3):
            rcopy(
                outb.at[c, mates[m]], out_hbm.at[:, lanes(mates[m], c)], out_send.at[c, m], out_recv.at[c, m], sibling
            ).wait_recv()
        out_own(c).wait()
    for r in regions:
        gather_end(r)
    for c in range(CHUNKS):
        sent += inbound(c) + edge_copies(c) + outbound(c)
    for copy in sent:
        copy.wait_send()


def closing_kernel(grad_ref, ag_ref, small_ref, grad_out, mixes_out, taps_out, gain_out, *, mix_scale, tok_scale):
    grad_out[...] = grad_ref[...]
    for m in range(mixes_out.shape[0]):
        for side in range(2):
            part = ag_ref[(2 * m + side) * T : (2 * m + side + 1) * T, :].astype(F32)
            mixes_out[m, :, side * LANES : (side + 1) * LANES] = part * mix_scale
    for i in range(D // LANES):
        part = small_ref[i // CHUNKS, i % CHUNKS] * tok_scale
        taps_out[:, i * LANES : (i + 1) * LANES] = part[:3]
        gain_out[i : i + 1, :] = part[3:4]


def local(tokens, cotangent, conv_taps, block_mixes, gate_gain):
    slabs = lax.axis_size("dp")
    tok_scale = 1.0 / math.sqrt(slabs * lax.axis_size("seq") * T)
    mix_scale = 1.0 / math.sqrt(slabs * lax.axis_size("seq") * D)
    small = (CHUNKS, 8, LANES)
    dma = pltpu.SemaphoreType.DMA
    wide = (T, WIDE)
    scratch = [
        *[pltpu.VMEM((CHUNKS, 4, T, LANES), BF16)] * 2,
        pltpu.VMEM((4, EDGE, QUARTER), BF16),
        pltpu.VMEM((CHUNKS, T + 16, WIDE), F32),
        pltpu.VMEM(wide, BF16),
        pltpu.VMEM((2 * T, WIDE), BF16),
        pltpu.VMEM((CHUNKS, *wide), F32),
        pltpu.VMEM((2 * T, WIDE), BF16),
        pltpu.VMEM((2 * T, WIDE), BF16),
        pltpu.VMEM(wide, BF16),
        pltpu.VMEM(wide, BF16),
        pltpu.VMEM((2 * T, WIDE), BF16),
        pltpu.VMEM(wide, BF16),
        pltpu.VMEM((CHUNKS, *wide), F32),
        pltpu.VMEM((CHUNKS, T + 16, WIDE), F32),
        pltpu.VMEM((CHUNKS, T, WIDE), F32),
        pltpu.VMEM((CHUNKS, 4, T, LANES), BF16),
        *[pltpu.VMEM((CHUNKS, 4, EDGE, LANES), BF16)] * 2,
        pltpu.VMEM((8, D), F32),
        pltpu.VMEM((3, D), BF16),
        pltpu.VMEM((6, T, T), BF16),
        *[pltpu.VMEM((T, n * T), BF16) for n in (1, 2, 1, 2, 1, 2, 1, 2)],
        pltpu.VMEM((ROWS, LANES), F32),
        pltpu.VMEM((PX, LANES), F32),
        *[pltpu.VMEM((HALF, LANES), BF16)] * 2,
        *[pltpu.VMEM((XS - 1, PX, LANES), BF16)] * 2,
        pltpu.VMEM((PX, LANES), BF16),
        pltpu.VMEM((YS - 1, PY, LANES), BF16),
        pltpu.VMEM((ZS, PY, LANES), BF16),
        *[pltpu.VMEM(small, F32)] * 2,
        *[pltpu.VMEM((4, *small), F32)] * 3,
        dma((2,)),
        *[dma((2, CHUNKS, 3))] * 2, dma((2, CHUNKS)),
        *[dma((4,))] * 2,
        *[dma((CHUNKS, 4))] * 2,
        *[dma((CHUNKS, 3))] * 2, dma((CHUNKS,)),
        *[dma((len(REGIONS),))] * 2,
        *[dma((len(REGIONS), XS - 1))] * 2,
        *[dma((len(REGIONS), YS - 1))] * 2,
        *[dma((len(REGIONS), ZS - 1))] * 2,
        *[dma((len(REGIONS), YS - 1))] * 2,
        *[dma((len(REGIONS), XS - 1))] * 2,
        *[dma((len(REGIONS), XS))] * 2,
        dma((2,)),
        *[dma((3,))] * 8,
    ]
    vmem, hbm = pl.BlockSpec(memory_space=pltpu.VMEM), pl.BlockSpec(memory_space=pltpu.HBM)
    flops = 18 * 2 * T * T * D
    input_grad, mixes, small_sums = pl.pallas_call(
        kernel,
        out_shape=(
            jax.ShapeDtypeStruct((T, D), BF16),
            jax.ShapeDtypeStruct((ROWS, LANES), BF16),
            jax.ShapeDtypeStruct((4, *small), F32),
        ),
        in_specs=[hbm, hbm, hbm, hbm, vmem],
        out_specs=(pl.BlockSpec(memory_space=pl.ANY), vmem, vmem),
        scratch_shapes=scratch,
        compiler_params=pltpu.CompilerParams(
            collective_id=0, has_side_effects=True, vmem_limit_bytes=56 * 1024 * 1024
        ),
        cost_estimate=pl.CostEstimate(flops=flops, bytes_accessed=6 * T * D, transcendentals=T * D),
    )(tokens[0], cotangent[0], conv_taps, block_mixes, gate_gain.reshape(D // LANES, LANES))
    steps = 2
    fixed = lambda shape: pl.BlockSpec(shape, lambda i: (0,) * len(shape))
    input_grad, mixes_grad, taps_grad, gain_grad = pl.pallas_call(
        functools.partial(closing_kernel, mix_scale=mix_scale, tok_scale=tok_scale),
        grid=(steps,),
        out_shape=(
            jax.ShapeDtypeStruct((T, D), BF16),
            jax.ShapeDtypeStruct((6, T, T), F32),
            jax.ShapeDtypeStruct((3, D), F32),
            jax.ShapeDtypeStruct((D // LANES, LANES), F32),
        ),
        in_specs=[
            pl.BlockSpec((T, D // steps), lambda i: (0, i)),
            pl.BlockSpec((ROWS // steps, LANES), lambda i: (i, 0)),
            fixed((4, *small)),
        ],
        out_specs=(
            pl.BlockSpec((T, D // steps), lambda i: (0, i)),
            pl.BlockSpec((6 // steps, T, T), lambda i: (i, 0, 0)),
            fixed((3, D)),
            fixed((D // LANES, LANES)),
        ),
    )(input_grad, mixes, small_sums)
    return input_grad[None], mixes_grad, taps_grad, gain_grad.reshape(D)


def solution(mesh):
    placed = (P("dp", "seq", None), P("dp", "seq", None), P(), P(), P())
    return jax.shard_map(
        local,
        mesh=mesh,
        in_specs=placed,
        out_specs=(P("dp", "seq", None), P(), P(), P()),
        check_vma=False,
    )
```

```python
import functools
import math

import jax
import jax.numpy as jnp
from jax import lax
from jax.experimental import pallas as pl
from jax.experimental.pallas import tpu as pltpu
from jax.sharding import PartitionSpec as P

F32, BF16 = jnp.float32, jnp.bfloat16
MESH = pl.DeviceIdType.MESH

CORES, XS, YS, ZLO, ZHI = 2, 4, 8, 4, 2
ZS = ZLO * ZHI
T, D = 256, 1536
QUARTER = D // 4
LANES = 128
CHUNKS = QUARTER // LANES
WIDE = 4 * LANES
EDGE = 16
TILE = 16
ROWS = 6 * T * T // LANES
REGIONS = (16, 16, 16)
HALF, PX, PY = ROWS // CORES, ROWS // (CORES * XS), ROWS // (CORES * XS * YS)


def far(v):
    return jnp.concatenate([v[:, 2 * LANES :], v[:, : 2 * LANES]], axis=1)


def near(v):
    a, b, c, d = (v[:, i * LANES : (i + 1) * LANES] for i in range(4))
    return jnp.concatenate([b, a, d, c], axis=1)


def mm(a, b):
    return jnp.dot(a, b, preferred_element_type=F32)


def mm_nt(a, b):
    return lax.dot_general(a, b, (((1,), (1,)), ((), ())), preferred_element_type=F32)


def kernel(
    tok_hbm, cot_hbm, taps_hbm, mixes_hbm, gain_ref,
    out_hbm, ag, e_out,
    tok, cot, halo, pad, conv, gf2, h, f2, t2, s2, gt, gs2, g1, fourth,
    gcpad, ggg, outb, edge_out, edges, wts, taps_ref, mixes_ref,
    m0, m12, m3, m45, m0t, m12t, m3t, m45t,
    grads, own_x, core_out, core_in, x_out, x_in, y_out, y_in, z_in,
    e_own, e_core, e_x, e_y, e_z,
    param_sem, in_send, in_recv, in_local, halo_send, halo_recv, edge_send, edge_recv,
    out_send, out_recv, out_local, core_send, core_recv, x_send, x_recv, y_send, y_recv,
    z_send, z_recv, gy_send, gy_recv, gx_send, gx_recv, gc_send, gc_recv,
    ec_sem, ex_send, ex_recv, ey_send, ey_recv, ez_send, ez_recv, eq_send, eq_recv,
):
    dp, k = lax.axis_index("dp"), lax.axis_index("seq")
    core, x, z_hi = lax.rem(dp, CORES), lax.rem(lax.div(dp, CORES), XS), lax.div(dp, CORES * XS)
    y, z_lo = lax.rem(k, YS), lax.div(k, YS)
    z = z_hi * ZLO + z_lo
    yb, yp = lax.rem(y, 2), lax.div(y, 2)
    zb, zp = lax.div(z_lo, 2), lax.rem(z_lo, 2)
    q = yb + 2 * zb

    def at(core_=core, x_=x, y_=y, z_=z):
        return (lax.div(z_, ZLO) * (XS * CORES) + x_ * CORES + core_, lax.rem(z_, ZLO) * YS + y_)

    def in_group(yp_, zp_, quarter):
        return (dp, (zp_ + 2 * lax.div(quarter, 2)) * YS + 2 * yp_ + lax.rem(quarter, 2))

    last_y, first_y = yp == YS // 2 - 1, yp == 0
    next_yp, next_zp = lax.rem(yp + 1, YS // 2), jnp.where(last_y, 1 - zp, zp)
    prev_yp, prev_zp = lax.rem(yp + YS // 2 - 1, YS // 2), jnp.where(first_y, 1 - zp, zp)
    next_flip = jnp.where(last_y, zp, 0)
    prev_flip = jnp.where(first_y, 1 - zp, 0)
    has_prev = 1.0 - prev_flip.astype(F32)
    has_next = 1.0 - next_flip.astype(F32)

    mates = [lax.rem(q + m, 4) for m in range(1, 4)]

    def rcopy(src, dst, send, recv, device):
        return pltpu.make_async_remote_copy(
            src_ref=src, dst_ref=dst, send_sem=send, recv_sem=recv, device_id=device, device_id_type=MESH
        )

    def lanes(quarter, c):
        return pl.ds(pl.multiple_of(quarter * QUARTER + c * LANES, LANES), LANES)

    params = [
        pltpu.make_async_copy(src, dst, param_sem.at[i])
        for i, (src, dst) in enumerate(((mixes_hbm, mixes_ref), (taps_hbm, taps_ref)))
    ]
    for copy in params:
        copy.start()

    barrier = pltpu.get_barrier_semaphore()
    others = [in_group(yp, zp, 3 - q)]
    others += [in_group(next_yp, next_zp, m) for m in range(4)]
    others += [in_group(prev_yp, prev_zp, m) for m in range(4)]
    others += [at(core_=1 - core)]
    others += [at(x_=lax.rem(x + i, XS)) for i in range(1, XS)]
    others += [at(y_=lax.rem(y + i, YS)) for i in range(1, YS)]
    others += [at(z_=lax.rem(z + i, ZS)) for i in range(1, ZS)]
    for device in others:
        pl.semaphore_signal(barrier, inc=1, device_id=device, device_id_type=MESH)
    pl.semaphore_wait(barrier, len(others))

    halo_yp, halo_zp = jnp.where(yb == 1, next_yp, prev_yp), jnp.where(yb == 1, next_zp, prev_zp)
    halo_flip = jnp.where(yb == 1, next_flip, prev_flip)
    halo_half = lax.rem(zb + halo_flip, 2)
    halo_slot = (1 - yb) * 2 + halo_half
    halo_row = pl.multiple_of(yb * (T - EDGE), EDGE)
    halo_copies = [
        rcopy(
            tok_hbm.at[pl.ds(halo_row, EDGE), pl.ds(m * QUARTER, QUARTER)],
            halo.at[halo_slot],
            halo_send.at[m],
            halo_recv.at[halo_slot],
            in_group(halo_yp, halo_zp, m),
        )
        for m in range(4)
    ]

    def inbound(c):
        copies = []
        for m in (1, 2, 0):
            for a in range(2):
                src, dst = ((tok_hbm, tok), (cot_hbm, cot))[a]
                copies.append(
                    rcopy(
                        src.at[:, lanes(mates[m], c)],
                        dst.at[c, q],
                        in_send.at[a, c, m],
                        in_recv.at[a, c, 2 - m],
                        in_group(yp, zp, mates[m]),
                    )
                )
        return copies

    def local(c):
        return [
            pltpu.make_async_copy(src.at[:, lanes(q, c)], dst.at[c, q], in_local.at[a, c])
            for a, (src, dst) in enumerate(((tok_hbm, tok), (cot_hbm, cot)))
        ]

    for c in range(CHUNKS):
        for copy in inbound(c) + local(c) + (halo_copies if c == 0 else []):
            copy.start()

    def transposed(v):
        return v.astype(F32).T.astype(BF16)

    for copy in params:
        copy.wait()
    m0[...] = mixes_ref[0]
    m12[:, :T], m12[:, T:] = mixes_ref[1], mixes_ref[2]
    m3[...] = mixes_ref[3]
    m45[:, :T], m45[:, T:] = mixes_ref[4], mixes_ref[5]
    m0t[...] = transposed(mixes_ref[0])
    m12t[:, :T], m12t[:, T:] = transposed(mixes_ref[1]), transposed(mixes_ref[2])
    m3t[...] = transposed(mixes_ref[3])
    m45t[:, :T], m45t[:, T:] = transposed(mixes_ref[4]), transposed(mixes_ref[5])
    wts[0:3, :] = taps_ref[...].astype(F32)
    for i in range(D // LANES):
        wts[3:4, i * LANES : (i + 1) * LANES] = gain_ref[i : i + 1, :]
    grads[...] = jnp.zeros_like(grads)
    e_own[...] = jnp.zeros_like(e_own)

    def weights(c):
        w = wts[:, lanes(q, c)]
        w = jnp.concatenate([w] * 4, axis=1)
        return [w[i : i + 1] for i in range(4)]

    def fill_edges(ref, prev, nxt):
        body = ref[8 : 16, :], ref[T : T + 8, :]
        first, last = body[0][0:1], body[1][7:8]
        ref[7:8, :] = jnp.concatenate([prev[0], last[:, :LANES], prev[1], last[:, 2 * LANES : 3 * LANES]], axis=1)
        ref[T + 8 : T + 9, :] = jnp.concatenate(
            [first[:, LANES : 2 * LANES], nxt[0], first[:, 3 * LANES :], nxt[1]], axis=1
        )

    def mask_edges(prev, nxt):
        return [prev[0] * has_prev, prev[1]], [nxt[0], nxt[1] * has_next]

    def tile_rows(i):
        return pl.ds(pl.multiple_of(i * TILE, TILE), TILE)

    def window(ref, i):
        w = ref[pl.ds(pl.multiple_of(i * TILE, TILE), TILE + 16), :]
        return w[7 : 7 + TILE], w[8 : 8 + TILE], w[9 : 9 + TILE]

    def edge_copies(c):
        copies = []
        for half in range(2):
            for side, (yp_, zp_, flip) in enumerate(((next_yp, next_zp, next_flip), (prev_yp, prev_zp, prev_flip))):
                slot = side * 2 + lax.rem(half + flip, 2)
                copies.append(
                    rcopy(
                        edge_out.at[c, side * 2 + half],
                        edges.at[c, slot],
                        edge_send.at[c, side * 2 + half],
                        edge_recv.at[c, slot],
                        in_group(yp_, zp_, q),
                    )
                )
        return copies

    def edge_wait(c):
        for slot in range(4):
            rcopy(
                edge_out.at[c, slot], edges.at[c, slot], edge_send.at[c, slot], edge_recv.at[c, slot],
                in_group(next_yp, next_zp, q),
            ).wait_recv()

    def wait_inbound(c):
        for a in range(2):
            dst = (tok, cot)[a]
            for m in range(3):
                rcopy(
                    dst.at[c, q], dst.at[c, mates[m]], in_send.at[a, c, m], in_recv.at[a, c, m],
                    in_group(yp, zp, mates[m]),
                ).wait_recv()
        for copy in local(c):
            copy.wait()

    def chain(c):
        for b in range(4):
            pad[c, 8 : 8 + T, b * LANES : (b + 1) * LANES] = tok[c, b].astype(F32)
        chunk = pl.ds(pl.multiple_of(c * LANES, LANES), LANES)
        ends = [halo[s, :, chunk].astype(F32) for s in range(4)]
        fill_edges(
            pad.at[c], *mask_edges([ends[0][EDGE - 1 :], ends[1][EDGE - 1 :]], [ends[2][:1], ends[3][:1]])
        )
        w = weights(c)

        def before(i, carry):
            prev, cur, nxt = window(pad.at[c], i)
            rows = tile_rows(i)
            conv[rows, :] = (w[0] * prev + w[1] * cur + w[2] * nxt).astype(BF16)
            up = jnp.concatenate([cot[c, b, rows, :] for b in range(4)], axis=1).astype(F32)
            gate = w[3] * cur
            sig = 1.0 / (1.0 + jnp.exp(-gate))
            gf = (up * gate * sig).astype(BF16)
            gf2[rows, :] = gf
            gf2[pl.ds(pl.multiple_of(T + i * TILE, TILE), TILE), :] = near(gf)
            h[c, rows, :] = up * sig * (1.0 + gate * (1.0 - sig))
            return carry

        lax.fori_loop(0, T // TILE, before, 0)

        first = mm(m0[...], conv[...]).astype(BF16)
        f2[:T, :], f2[T:, :] = first, far(first)
        third_grad = mm(m45t[...], gf2[...]).astype(BF16)
        gt[...] = third_grad
        s2[...] = mm(m12[...], f2[...]).astype(BF16)
        second_grad = mm(m3t[...], gt[...]).astype(BF16)
        gs2[:T, :], gs2[T:, :] = second_grad, far(second_grad)
        third = mm(m3[...], s2[...]).astype(BF16)
        t2[:T, :], t2[T:, :] = third, near(third)
        g1[...] = mm(m12t[...], gs2[...]).astype(BF16)
        fourth[c] = mm(m45[...], t2[...])
        gc = mm(m0t[...], g1[...]).astype(BF16)
        gcpad[c, 8 : 8 + T, :] = gc.astype(F32)
        for half in range(2):
            odd = slice((2 * half + 1) * LANES, (2 * half + 2) * LANES)
            even = slice(2 * half * LANES, (2 * half + 1) * LANES)
            edge_out[c, half] = gc[T - EDGE :, odd]
            edge_out[c, 2 + half] = gc[:EDGE, even]
        for copy in edge_copies(c):
            copy.start()

        def add_grad(i, value):
            grads[2 * i * T : (2 * i + 1) * T, :] += value[:, :LANES]
            grads[(2 * i + 1) * T : (2 * i + 2) * T, :] += value[:, LANES:]

        add_grad(0, mm_nt(g1[...], conv[...]))
        add_grad(3, mm_nt(gt[...], s2[...]))
        both = mm_nt(gs2[:T, :], f2[...])
        add_grad(1, both[:, :T])
        add_grad(2, both[:, T:])
        both = mm_nt(gf2[:T, :], t2[...])
        add_grad(4, both[:, :T])
        add_grad(5, both[:, T:])

    def sums(c):
        w = weights(c)

        def after(i, carry):
            prev, cur, nxt = window(pad.at[c], i)
            rows = tile_rows(i)
            gg = h[c, rows, :] * fourth[c, rows, :]
            gc = gcpad[c, pl.ds(pl.multiple_of(8 + i * TILE, 8), TILE), :]
            ggg[c, rows, :] = gg * w[3]

            def fold(v):
                return v[:8] + v[8:]

            return tuple(
                have + fold(v) for have, v in zip(carry, (gc * prev, gc * cur, gc * nxt, gg * cur))
            )

        zero = jnp.zeros((8, WIDE), F32)
        totals = lax.fori_loop(0, T // TILE, after, (zero,) * 4)
        for j, total in enumerate(totals):
            row = jnp.sum(total, axis=0, keepdims=True)
            e_own[c, j : j + 1, :] = sum(row[:, b * LANES : (b + 1) * LANES] for b in range(4))

    def finish(c):
        edge_wait(c)
        ends = [edges[c, s].astype(F32) for s in range(4)]
        fill_edges(
            gcpad.at[c], *mask_edges([ends[0][EDGE - 1 :], ends[1][EDGE - 1 :]], [ends[2][:1], ends[3][:1]])
        )
        w = weights(c)

        def close(i, carry):
            prev, cur, nxt = window(gcpad.at[c], i)
            rows = tile_rows(i)
            out = (w[0] * nxt + w[1] * cur + w[2] * prev + ggg[c, rows, :]).astype(BF16)
            for b in range(4):
                outb[c, b, rows, :] = out[:, b * LANES : (b + 1) * LANES]
            return carry

        lax.fori_loop(0, T // TILE, close, 0)

    def outbound(c):
        return [
            rcopy(
                outb.at[c, mates[m]],
                out_hbm.at[:, lanes(q, c)],
                out_send.at[c, m],
                out_recv.at[c, 2 - m],
                in_group(yp, zp, mates[m]),
            )
            for m in (1, 2, 0)
        ]

    def out_own(c):
        return pltpu.make_async_copy(outb.at[c, q], out_hbm.at[:, lanes(q, c)], out_local.at[c])

    def send_out(c):
        for copy in outbound(c):
            copy.start()
        out_own(c).start()

    for slot in range(4):
        rcopy(
            tok_hbm.at[pl.ds(0, EDGE), pl.ds(0, QUARTER)], halo.at[slot], halo_send.at[slot], halo_recv.at[slot],
            in_group(next_yp, next_zp, q),
        ).wait_recv()

    def step(c, carry):
        wait_inbound(c)
        chain(c)

        return carry

    lax.fori_loop(0, CHUNKS, step, 0)

    sibling = at(core_=1 - core)
    x_mates = [lax.rem(x + i, XS) for i in range(1, XS)]
    y_mates = [lax.rem(y + i, YS) for i in range(1, YS)]
    z_mates = [lax.rem(z + i, ZS) for i in range(1, ZS)]

    def rows_of(start, size):
        return pl.ds(pl.multiple_of(start, EDGE), size)

    sent = list(halo_copies)

    def begin(copies):
        for copy in copies:
            copy.start()
        sent.extend(copies)
        return copies

    def slot_wait(ref, slot, send, recv):
        rcopy(ref.at[slot], ref.at[slot], send, recv, sibling).wait_recv()

    def offset(r):
        return CORES * XS * YS * sum(REGIONS[:r]) // CORES

    def sizes(r):
        return offset(r), YS * REGIONS[r], REGIONS[r]

    def core_stage(r):
        base, px, py = sizes(r)
        there = pl.ds(base, XS * px)
        core_out[there, :] = grads[rows_of((1 - core) * HALF + base, XS * px), :].astype(BF16)
        return begin([rcopy(core_out.at[there], core_in.at[there], core_send.at[r], core_recv.at[r], sibling)])

    def x_stage(r, copies):
        base, px, py = sizes(r)
        for copy in copies:
            copy.wait_recv()
        rows = pl.ds(base // XS, px)
        started = []
        for i, other in enumerate(x_mates):
            part = grads[rows_of(core * HALF + base + other * px, px), :]
            x_out[i, rows, :] = (part + core_in[rows_of(base + other * px, px), :].astype(F32)).astype(BF16)
            started += begin(
                [rcopy(x_out.at[i, rows], x_in.at[i, rows], x_send.at[r, i], x_recv.at[r, i], at(x_=other))]
            )
        part = grads[rows_of(core * HALF + base + x * px, px), :]
        own_x[rows, :] = part + core_in[rows_of(base + x * px, px), :].astype(F32)
        return started

    def y_stage(r, copies):
        base, px, py = sizes(r)
        for copy in copies:
            copy.wait_recv()
        rows = pl.ds(base // XS, px)
        own_x[rows, :] += sum(x_in[i, rows, :].astype(F32) for i in range(XS - 1))
        y_out[rows, :] = own_x[rows, :].astype(BF16)
        there = pl.ds(base // (XS * YS), py)
        return begin(
            [
                rcopy(
                    y_out.at[rows_of(base // XS + other * py, py)],
                    y_in.at[i, there],
                    y_send.at[r, i],
                    y_recv.at[r, i],
                    at(y_=other),
                )
                for i, other in enumerate(y_mates)
            ]
        )

    def z_stage(r, copies):
        base, px, py = sizes(r)
        for copy in copies:
            copy.wait_recv()
        rows = pl.ds(base // (XS * YS), py)
        total = own_x[rows_of(base // XS + y * py, py), :]
        total = total + sum(y_in[i, rows, :].astype(F32) for i in range(YS - 1))
        z_in[z, rows, :] = total.astype(BF16)
        return begin(
            [
                rcopy(z_in.at[z, rows], z_in.at[z, rows], z_send.at[r, i], z_recv.at[r, i], at(z_=other))
                for i, other in enumerate(z_mates)
            ]
        )

    def gather_y(r):
        base, px, py = sizes(r)
        rows = pl.ds(base // (XS * YS), py)
        for i in range(ZS - 1):
            there = z_in.at[lax.rem(z + ZS - 1 - i, ZS), rows]
            rcopy(there, there, z_send.at[r, i], z_recv.at[r, i], sibling).wait_recv()
        total = z_in[0, rows, :].astype(F32)
        for i in range(1, ZS):
            total = total + z_in[i, rows, :].astype(F32)
        own = rows_of(core * HALF + base + x * px + y * py, py)
        ag[own, :] = total.astype(BF16)
        begin(
            [
                rcopy(ag.at[own], ag.at[own], gy_send.at[r, i], gy_recv.at[r, i], at(y_=other))
                for i, other in enumerate(y_mates)
            ]
        )

    def gather_x(r):
        base, px, py = sizes(r)
        for i in range(YS - 1):
            there = ag.at[rows_of(core * HALF + base + x * px + lax.rem(y + YS - 1 - i, YS) * py, py)]
            rcopy(there, there, gy_send.at[r, i], gy_recv.at[r, i], sibling).wait_recv()
        mine = ag.at[rows_of(core * HALF + base + x * px, px)]
        begin(
            [
                rcopy(mine, mine, gx_send.at[r, i], gx_recv.at[r, i], at(x_=other))
                for i, other in enumerate(x_mates)
            ]
            + [rcopy(mine, mine, gc_send.at[r, 0], gc_recv.at[r, 0], sibling)]
        )

    def gather_core(r):
        base, px, py = sizes(r)
        for i in range(XS - 1):
            there = ag.at[rows_of(core * HALF + base + lax.rem(x + XS - 1 - i, XS) * px, px)]
            rcopy(there, there, gx_send.at[r, i], gx_recv.at[r, i], sibling).wait_recv()
            begin([rcopy(there, there, gc_send.at[r, i + 1], gc_recv.at[r, i + 1], sibling)])

    def gather_end(r):
        base, px, py = sizes(r)
        for i in range(XS):
            there = ag.at[rows_of((1 - core) * HALF + base + lax.rem(x + XS - i, XS) * px, px)]
            rcopy(there, there, gc_send.at[r, i], gc_recv.at[r, i], sibling).wait_recv()

    regions = range(len(REGIONS))
    flights = [core_stage(r) for r in regions]
    for c in range(CHUNKS):
        sums(c)
    e_core_copy = begin([rcopy(e_own, e_core, ec_sem.at[0], ec_sem.at[1], sibling)])[0]
    flights = [x_stage(r, flights[r]) for r in regions]
    for past in range(CHUNKS - 1):
        finish(past)
        send_out(past)
    e_core_copy.wait_recv()
    e_x[x] = e_own[...] + e_core[...]
    begin(
        [rcopy(e_x.at[x], e_x.at[x], ex_send.at[i], ex_recv.at[i], at(x_=other)) for i, other in enumerate(x_mates)]
    )
    finish(CHUNKS - 1)
    flights = [y_stage(r, flights[r]) for r in regions]

    for i in range(XS - 1):
        slot_wait(e_x, lax.rem(x + XS - 1 - i, XS), ex_send.at[i], ex_recv.at[i])
    e_y[yp] = e_x[0] + e_x[1] + e_x[2] + e_x[3]
    begin(
        [
            rcopy(e_y.at[yp], e_y.at[yp], ey_send.at[i], ey_recv.at[i], at(y_=lax.rem(y + 2 * (i + 1), YS)))
            for i in range(3)
        ]
    )
    for r in regions:
        z_stage(r, flights[r])
    send_out(CHUNKS - 1)

    for i in range(3):
        slot_wait(e_y, lax.rem(yp + 3 - i, 4), ey_send.at[i], ey_recv.at[i])
    ez_me = z_hi * 2 + zp
    e_z[ez_me] = e_y[0] + e_y[1] + e_y[2] + e_y[3]

    def ez_device(slot):
        return at(z_=lax.div(slot, 2) * ZLO + 2 * zb + lax.rem(slot, 2))

    begin(
        [
            rcopy(e_z.at[ez_me], e_z.at[ez_me], ez_send.at[i], ez_recv.at[i], ez_device(lax.rem(ez_me + i + 1, 4)))
            for i in range(3)
        ]
    )
    for r in regions:
        gather_y(r)

    for i in range(3):
        slot_wait(e_z, lax.rem(ez_me + 3 - i, 4), ez_send.at[i], ez_recv.at[i])
    e_out[q] = e_z[0] + e_z[1] + e_z[2] + e_z[3]
    begin(
        [
            rcopy(e_out.at[q], e_out.at[q], eq_send.at[i], eq_recv.at[i], in_group(yp, zp, mates[i]))
            for i in range(3)
        ]
    )
    for r in regions:
        gather_x(r)
    for r in regions:
        gather_core(r)

    for i in range(3):
        slot_wait(e_out, mates[2 - i], eq_send.at[i], eq_recv.at[i])
    for c in range(CHUNKS):
        for m in range(3):
            rcopy(
                outb.at[c, mates[m]], out_hbm.at[:, lanes(mates[m], c)], out_send.at[c, m], out_recv.at[c, m], sibling
            ).wait_recv()
        out_own(c).wait()
    for r in regions:
        gather_end(r)
    for c in range(CHUNKS):
        sent += inbound(c) + edge_copies(c) + outbound(c)
    for copy in sent:
        copy.wait_send()


def closing_kernel(grad_ref, ag_ref, small_ref, grad_out, mixes_out, taps_out, gain_out, *, mix_scale, tok_scale):
    grad_out[...] = grad_ref[...]
    for m in range(mixes_out.shape[0]):
        for side in range(2):
            part = ag_ref[(2 * m + side) * T : (2 * m + side + 1) * T, :].astype(F32)
            mixes_out[m, :, side * LANES : (side + 1) * LANES] = part * mix_scale
    for i in range(D // LANES):
        part = small_ref[i // CHUNKS, i % CHUNKS] * tok_scale
        taps_out[:, i * LANES : (i + 1) * LANES] = part[:3]
        gain_out[i : i + 1, :] = part[3:4]


def local(tokens, cotangent, conv_taps, block_mixes, gate_gain):
    slabs = lax.axis_size("dp")
    tok_scale = 1.0 / math.sqrt(slabs * lax.axis_size("seq") * T)
    mix_scale = 1.0 / math.sqrt(slabs * lax.axis_size("seq") * D)
    small = (CHUNKS, 8, LANES)
    dma = pltpu.SemaphoreType.DMA
    wide = (T, WIDE)
    scratch = [
        *[pltpu.VMEM((CHUNKS, 4, T, LANES), BF16)] * 2,
        pltpu.VMEM((4, EDGE, QUARTER), BF16),
        pltpu.VMEM((CHUNKS, T + 16, WIDE), F32),
        pltpu.VMEM(wide, BF16),
        pltpu.VMEM((2 * T, WIDE), BF16),
        pltpu.VMEM((CHUNKS, *wide), F32),
        pltpu.VMEM((2 * T, WIDE), BF16),
        pltpu.VMEM((2 * T, WIDE), BF16),
        pltpu.VMEM(wide, BF16),
        pltpu.VMEM(wide, BF16),
        pltpu.VMEM((2 * T, WIDE), BF16),
        pltpu.VMEM(wide, BF16),
        pltpu.VMEM((CHUNKS, *wide), F32),
        pltpu.VMEM((CHUNKS, T + 16, WIDE), F32),
        pltpu.VMEM((CHUNKS, T, WIDE), F32),
        pltpu.VMEM((CHUNKS, 4, T, LANES), BF16),
        *[pltpu.VMEM((CHUNKS, 4, EDGE, LANES), BF16)] * 2,
        pltpu.VMEM((8, D), F32),
        pltpu.VMEM((3, D), BF16),
        pltpu.VMEM((6, T, T), BF16),
        *[pltpu.VMEM((T, n * T), BF16) for n in (1, 2, 1, 2, 1, 2, 1, 2)],
        pltpu.VMEM((ROWS, LANES), F32),
        pltpu.VMEM((PX, LANES), F32),
        *[pltpu.VMEM((HALF, LANES), BF16)] * 2,
        *[pltpu.VMEM((XS - 1, PX, LANES), BF16)] * 2,
        pltpu.VMEM((PX, LANES), BF16),
        pltpu.VMEM((YS - 1, PY, LANES), BF16),
        pltpu.VMEM((ZS, PY, LANES), BF16),
        *[pltpu.VMEM(small, F32)] * 2,
        *[pltpu.VMEM((4, *small), F32)] * 3,
        dma((2,)),
        *[dma((2, CHUNKS, 3))] * 2, dma((2, CHUNKS)),
        *[dma((4,))] * 2,
        *[dma((CHUNKS, 4))] * 2,
        *[dma((CHUNKS, 3))] * 2, dma((CHUNKS,)),
        *[dma((len(REGIONS),))] * 2,
        *[dma((len(REGIONS), XS - 1))] * 2,
        *[dma((len(REGIONS), YS - 1))] * 2,
        *[dma((len(REGIONS), ZS - 1))] * 2,
        *[dma((len(REGIONS), YS - 1))] * 2,
        *[dma((len(REGIONS), XS - 1))] * 2,
        *[dma((len(REGIONS), XS))] * 2,
        dma((2,)),
        *[dma((3,))] * 8,
    ]
    vmem, hbm = pl.BlockSpec(memory_space=pltpu.VMEM), pl.BlockSpec(memory_space=pltpu.HBM)
    flops = 18 * 2 * T * T * D
    input_grad, mixes, small_sums = pl.pallas_call(
        kernel,
        out_shape=(
            jax.ShapeDtypeStruct((T, D), BF16),
            jax.ShapeDtypeStruct((ROWS, LANES), BF16),
            jax.ShapeDtypeStruct((4, *small), F32),
        ),
        in_specs=[hbm, hbm, hbm, hbm, vmem],
        out_specs=(pl.BlockSpec(memory_space=pl.ANY), vmem, vmem),
        scratch_shapes=scratch,
        compiler_params=pltpu.CompilerParams(
            collective_id=0, has_side_effects=True, vmem_limit_bytes=56 * 1024 * 1024
        ),
        cost_estimate=pl.CostEstimate(flops=flops, bytes_accessed=6 * T * D, transcendentals=T * D),
    )(tokens[0], cotangent[0], conv_taps, block_mixes, gate_gain.reshape(D // LANES, LANES))
    steps = 2
    fixed = lambda shape: pl.BlockSpec(shape, lambda i: (0,) * len(shape))
    input_grad, mixes_grad, taps_grad, gain_grad = pl.pallas_call(
        functools.partial(closing_kernel, mix_scale=mix_scale, tok_scale=tok_scale),
        grid=(steps,),
        out_shape=(
            jax.ShapeDtypeStruct((T, D), BF16),
            jax.ShapeDtypeStruct((6, T, T), F32),
            jax.ShapeDtypeStruct((3, D), F32),
            jax.ShapeDtypeStruct((D // LANES, LANES), F32),
        ),
        in_specs=[
            pl.BlockSpec((T, D // steps), lambda i: (0, i)),
            pl.BlockSpec((ROWS // steps, LANES), lambda i: (i, 0)),
            fixed((4, *small)),
        ],
        out_specs=(
            pl.BlockSpec((T, D // steps), lambda i: (0, i)),
            pl.BlockSpec((6 // steps, T, T), lambda i: (i, 0, 0)),
            fixed((3, D)),
            fixed((D // LANES, LANES)),
        ),
    )(input_grad, mixes, small_sums)
    return input_grad[None], mixes_grad, taps_grad, gain_grad.reshape(D)


def solution(mesh):
    placed = (P("dp", "seq", None), P("dp", "seq", None), P(), P(), P())
    return jax.shard_map(
        local,
        mesh=mesh,
        in_specs=placed,
        out_specs=(P("dp", "seq", None), P(), P(), P()),
        check_vma=False,
    )
```
